128 devices in a mesh: section: 4 (over x), dp: 32 (over z, y, core).
Axes of the slice: x: 4, y: 4, z: 4, core: 2. Of those that a mesh axis runs over, the one named last changes fastest.
Arguments:
- tokens: bfloat16 [2, 4096, 5120], P(None, 'dp'), may hold values from -26 to 26
- cotangent: bfloat16 [2, 4096, 5120], P(None, 'dp'), may hold values from -0.59765625 to 0.59765625
- norm_gain: float32 [4, 5120], P('section'), may hold values from 0.25 to 1.75
- value_weight: bfloat16 [4, 5120, 512], P('section'), may hold values from -2 to 2
- out_weight: bfloat16 [4, 512, 5120], P('section'), may hold values from -2 to 2
- adapter_down: bfloat16 [4, 128, 5120, 64], P('section', None, 'dp'), may hold values from -0.078125 to 0.078125
- adapter_up: bfloat16 [4, 128, 512, 64], P('section', None, 'dp'), may hold values from -0.75 to 0.75
- criterion: int32 [2, 32], replicated, may hold values from 0 to 127
- slot_of: int32 [128], replicated, may hold values from 0 to 127, each once
Outputs:
- grad_down: float32 [4, 128, 5120, 64], P('section', None, 'dp')
- grad_up: float32 [4, 128, 512, 64], P('section', None, 'dp')
The draws below stay inside these ranges and needn't reach their ends.
Inputs may be any that keep to these rules, and one draw needn't show every extreme that they name: Each block's criterion id; some criteria are far more common than others, and one criterion may serve many blocks. `slot_of`: each of 0 to 127 once.
All inputs are finite; a program needn't handle non-finite values.
Results may differ from the reference program's by a relative error of at most 0.015.
Values may be sent and summed in bfloat16 or wider, within the bound.
A program may use at most 192 MiB of HBM per device.

```python
import math
import jax
import jax.numpy as jnp
import numpy as np
from jax import lax

D = 5120
KV = 512
R = 64
CRIT = 128
MB = 2
BLOCKS = 32
TOKENS = 4096
SECTIONS = 4


def shared_panel(key):
    return jnp.clip(jax.random.normal(key, (SECTIONS, D, KV), jnp.float32), -5.0, 5.0)


def draw_tokens(key, part):
    key = jax.random.fold_in(key, 11)
    features = jnp.arange(D, dtype=jnp.int32)
    residue = jax.random.randint(jax.random.fold_in(key, 1), (), 0, 8)
    period = jnp.where(features % 8 == residue, 2.0, 1.0).astype(jnp.float32)
    roughness = jnp.exp(jax.random.uniform(jax.random.fold_in(key, 2), (D,), jnp.float32, math.log(0.6), math.log(1.6)))
    base_draw = jnp.clip(jax.random.normal(jax.random.fold_in(key, 3), (MB, TOKENS, D), jnp.float32), -4.0, 4.0)
    row_scale = jnp.exp(jax.random.uniform(jax.random.fold_in(key, 4), (MB, TOKENS, 1), jnp.float32, math.log(0.5), math.log(2.0)))
    return (base_draw * row_scale * (period * roughness)).astype(jnp.bfloat16)


def draw_value_weight(key, part):
    common = shared_panel(key)
    key = jax.random.fold_in(key, 21)
    own_part = jnp.clip(jax.random.normal(key, (SECTIONS, D, KV), jnp.float32), -5.0, 5.0)
    return ((0.95 * common + 0.3122 * own_part) / math.sqrt(D)).astype(jnp.bfloat16)


def draw_out_weight(key, part):
    common = jnp.swapaxes(shared_panel(key), 1, 2)
    key = jax.random.fold_in(key, 31)
    own_part = jnp.clip(jax.random.normal(key, (SECTIONS, KV, D), jnp.float32), -5.0, 5.0)
    return ((0.95 * common + 0.3122 * own_part) / math.sqrt(KV)).astype(jnp.bfloat16)


def with_ends(entries, key, smallest, largest):
    spot = [jax.random.randint(jax.random.fold_in(key, axis), (), 0, length) for axis, length in enumerate(entries.shape)]
    longest = entries.shape.index(max(entries.shape))
    beside = spot[:longest] + [(spot[longest] + 1) % entries.shape[longest]] + spot[longest + 1:]
    return entries.at[tuple(spot)].set(smallest).at[tuple(beside)].set(largest)


def level_of(own_key, shape, shards, least, largest):
    gain = 1.0
    for position, parts in shards:
        steps = jax.random.uniform(jax.random.fold_in(jax.random.fold_in(own_key, 6), position), (parts,), jnp.float32, least / len(shards), largest / len(shards))
        gain = gain * jnp.repeat(jnp.exp(steps), shape[position] // parts).reshape((-1,) + (1,) * (len(shape) - 1 - position))
    return gain


def cumulative_ranks(number_of, slope):
    weights = [(1 << 20) // math.isqrt(grade ** slope) + 1 for grade in range(1, number_of + 1)]
    width = 1 + sum(weights) // (1 << 30)
    return np.cumsum(np.array([max(1, weight // width) for weight in weights]))


def skewed_ids(key, extent, number_of, lean):
    table = cumulative_ranks(number_of, lean)
    ticket = jax.random.randint(jax.random.fold_in(key, 1), extent, 0, int(table[number_of - 1]))
    grade = jnp.searchsorted(jnp.asarray(table, jnp.int32), ticket, side="right")
    return jax.random.permutation(jax.random.fold_in(key, 2), number_of)[grade].astype(jnp.int32)


def bell_draw(own_key, extent, width, most, cuts=(), held_as=jnp.bfloat16):
    result = width * jax.random.normal(own_key, extent, jnp.float32)
    if cuts:
        result = result * level_of(own_key, extent, cuts, -0.22, 0.18)
    return jnp.clip(result, -most, most).astype(held_as)


def setup_inputs(seed: int = 0) -> dict:
    seeds = jax.random.split(jax.random.key(seed), 10)
    tokens = draw_tokens(jax.random.fold_in(seeds[9], 71), 0)
    cotangent = bell_draw(seeds[1], (MB, TOKENS, D), 0.1, 0.59765625, ((1, 32),))
    norm_gain = jnp.clip(1.0 + 0.15 * jax.random.normal(seeds[2], (SECTIONS, D), jnp.float32), 0.25, 1.75)
    value_weight = draw_value_weight(jax.random.fold_in(seeds[9], 71), 0)
    out_weight = draw_out_weight(jax.random.fold_in(seeds[9], 71), 0)
    adapter_down = bell_draw(seeds[5], (SECTIONS, CRIT, D, R), D ** -0.5, 0.078125, ((0, 4), (2, 32)))
    adapter_up = bell_draw(seeds[6], (SECTIONS, CRIT, KV, R), R ** -0.5, 0.75, ((0, 4), (2, 32)))
    criterion = with_ends(skewed_ids(seeds[7], (MB, BLOCKS), CRIT, 2), jax.random.fold_in(seeds[7], 3), 0, CRIT - 1).astype(jnp.int32)
    slot_of = jax.random.permutation(seeds[8], CRIT).astype(jnp.int32)
    return dict(tokens=tokens, cotangent=cotangent, norm_gain=norm_gain, value_weight=value_weight, out_weight=out_weight, adapter_down=adapter_down, adapter_up=adapter_up, criterion=criterion, slot_of=slot_of)


epsilon = 1e-06

def normalize(hidden, gains):
    widened = hidden.astype(jnp.float32)
    inverse = lax.rsqrt(lax.optimization_barrier(jnp.mean(widened * widened, axis=-1, keepdims=True)) + epsilon)
    return ((widened * inverse * gains).astype(jnp.bfloat16), inverse)

def forward_section(hidden, gains, w_value, w_out, down_panel, up_panel):
    normed, inverse = normalize(hidden, gains)
    blocks = down_panel.shape[0]
    grouped = normed.reshape(blocks, -1, normed.shape[-1]).astype(jnp.float32)
    low_rank = jnp.einsum('btd,bdr->btr', grouped, down_panel.astype(jnp.float32)).astype(jnp.bfloat16)
    lifted = jnp.einsum('btr,bkr->btk', low_rank.astype(jnp.float32), up_panel.astype(jnp.float32))
    lifted = lifted.reshape(hidden.shape[0], -1)
    values = (jnp.dot(normed, w_value, preferred_element_type=jnp.float32) + lifted).astype(jnp.bfloat16)
    mixed = hidden.astype(jnp.float32) + jnp.dot(values, w_out, preferred_element_type=jnp.float32)
    return mixed.astype(jnp.bfloat16)

def backward_section(hidden, gradient, gains, w_value, w_out, down_panel, up_panel):
    normed, inverse = normalize(hidden, gains)
    blocks = down_panel.shape[0]
    grouped = normed.reshape(blocks, -1, normed.shape[-1]).astype(jnp.float32)
    low_rank = jnp.einsum('btd,bdr->btr', grouped, down_panel.astype(jnp.float32)).astype(jnp.bfloat16)
    grad_value = jnp.dot(gradient, jnp.transpose(w_out), preferred_element_type=jnp.float32).astype(jnp.bfloat16)
    grad_groups = grad_value.reshape(blocks, -1, grad_value.shape[-1]).astype(jnp.float32)
    grad_low = jnp.einsum('btk,bkr->btr', grad_groups, up_panel.astype(jnp.float32)).astype(jnp.bfloat16)
    pulled = jnp.einsum('btr,bdr->btd', grad_low.astype(jnp.float32), down_panel.astype(jnp.float32))
    pulled = pulled.reshape(hidden.shape[0], -1)
    grad_norm = jnp.dot(grad_value, jnp.transpose(w_value), preferred_element_type=jnp.float32) + pulled
    scaled = grad_norm * gains
    widened = hidden.astype(jnp.float32)
    moment = lax.optimization_barrier(jnp.mean(scaled * widened, axis=-1, keepdims=True))
    grad_hidden = gradient.astype(jnp.float32) + inverse * scaled - widened * inverse * inverse * inverse * moment
    part_down = jnp.einsum('btd,btr->bdr', grouped, grad_low.astype(jnp.float32))
    part_up = jnp.einsum('btk,btr->bkr', grad_groups, low_rank.astype(jnp.float32))
    return (grad_hidden.astype(jnp.bfloat16), part_down, part_up)

def reference(tokens, cotangent, norm_gain, value_weight, out_weight, adapter_down, adapter_up, criterion, slot_of):
    slots = slot_of[criterion]
    grad_down = jnp.zeros(adapter_down.shape, jnp.float32)
    grad_up = jnp.zeros(adapter_up.shape, jnp.float32)
    for micro_index in range(MB):
        picked = slots[micro_index]
        inputs = []
        hidden = tokens[micro_index]
        for layer_index in range(SECTIONS):
            inputs.append(hidden)
            hidden = forward_section(hidden, norm_gain[layer_index], value_weight[layer_index], out_weight[layer_index], adapter_down[layer_index][picked], adapter_up[layer_index][picked])
        gradient = cotangent[micro_index]
        for layer_index in reversed(range(SECTIONS)):
            gradient, part_down, part_up = backward_section(inputs[layer_index], gradient, norm_gain[layer_index], value_weight[layer_index], out_weight[layer_index], adapter_down[layer_index][picked], adapter_up[layer_index][picked])
            grad_down = grad_down.at[layer_index, picked].add(part_down)
            grad_up = grad_up.at[layer_index, picked].add(part_up)
    return (grad_down, grad_up)
```

```python
import jax
import jax.numpy as jnp
from jax import lax
from jax.experimental import pallas as pl
from jax.experimental.pallas import tpu as pltpu
from jax.sharding import PartitionSpec as P

EPSILON = 1e-06
CHUNK = 32
TILE = 512
GROUP = 16
LANES = 128
BF16 = jnp.bfloat16
F32 = jnp.float32


def dot(left, right):
    return jnp.dot(left, right, preferred_element_type=F32)


def dot_nt(left, right):
    return lax.dot_general(left, right, (((1,), (1,)), ((), ())), preferred_element_type=F32)


def dot_tn(left, right):
    return lax.dot_general(left, right, (((0,), (0,)), ((), ())), preferred_element_type=F32)


def swap_halves(value):
    half = value.shape[-1] // 2
    return jnp.concatenate([value[:, half:], value[:, :half]], axis=1)


def fill_picks(picks, criterion, slot_of):
    micro, blocks = criterion.shape
    lanes = lax.broadcasted_iota(jnp.int32, (1, picks.shape[1]), 1)
    for index in range(micro * blocks):
        slot = slot_of[criterion[index // blocks, index % blocks]]
        picks[index : index + 1, :] = jnp.where(lanes == slot, 1.0, 0.0)


def chain_kernel(
    tokens,
    cotangent,
    gains,
    w_value,
    w_out,
    down,
    up,
    criterion,
    slot_of,
    grad_recv,
    value_ref,
    out_ref,
    down_ref,
    up_ref,
    picks,
    h_in,
    h_out,
    g_in,
    g_out,
    normed,
    inverse,
    value_grad,
    low,
    low_grad,
    scaled,
    panel_send,
    panel_recv,
    panel_down,
    panel_up,
    product_down,
    product_up,
    grad_send,
    load_sem,
    h_send_sem,
    h_recv_sem,
    g_send_sem,
    g_recv_sem,
    panel_send_sem,
    panel_recv_sem,
    grad_send_sem,
    grad_recv_sem,
):
    sections = lax.axis_size("section")
    peers = lax.axis_size("dp")
    section = lax.axis_index("section")
    me = lax.axis_index("dp")
    micro = criterion.shape[0]
    rows, width = h_in.shape
    block = rows // micro
    chunks = rows // CHUNK
    per_block = block // CHUNK
    slots = picks.shape[1]
    feature_rows = down.shape[0]
    value_rows = up.shape[0]
    down_half = feature_rows // 2
    up_half = value_rows // 2
    packed = panel_send.shape[2]
    tiles = [slice(start, start + TILE) for start in range(0, width, TILE)]
    first = section == 0
    last = section == sections - 1

    loads = [
        pltpu.make_async_copy(source, target, load_sem.at[place])
        for place, (source, target) in enumerate(
            [(down, down_ref), (up, up_ref), (w_value, value_ref), (w_out, out_ref)]
        )
    ]
    for load in loads:
        load.start()

    def chunk_rows(c):
        return pl.ds(pl.multiple_of(c * CHUNK, CHUNK), CHUNK)

    @pl.when(first)
    def _():
        for c in range(chunks):
            part = pl.ds(c * CHUNK, CHUNK)
            pltpu.make_async_copy(tokens.at[part], h_in.at[part], h_recv_sem.at[c]).start()

    @pl.when(last)
    def _():
        for c in range(chunks):
            part = pl.ds(c * CHUNK, CHUNK)
            pltpu.make_async_copy(cotangent.at[part], g_in.at[part], g_recv_sem.at[c]).start()

    barrier = pltpu.get_barrier_semaphore()

    def greet(k, carry):
        pl.semaphore_signal(
            barrier,
            inc=1,
            device_id={"dp": lax.rem(me + k, peers)},
            device_id_type=pl.DeviceIdType.MESH,
        )
        return carry

    lax.fori_loop(1, peers, greet, 0)
    for step in (1, sections - 1):
        pl.semaphore_signal(
            barrier,
            inc=1,
            device_id={"section": lax.rem(section + step, sections)},
            device_id_type=pl.DeviceIdType.MESH,
        )

    fill_picks(picks, criterion, slot_of)
    chosen = picks[...].astype(BF16)
    loads[0].wait()
    loads[1].wait()
    for start in range(0, down_half, GROUP):
        pair = jnp.concatenate(
            [down_ref[start : start + GROUP], down_ref[down_half + start : down_half + start + GROUP]],
            axis=1,
        )
        found = dot_nt(chosen, pair.reshape(GROUP * LANES, slots))
        found = found.reshape(micro, peers, GROUP, LANES).astype(BF16)
        panel_send[:, :, start : start + GROUP, :] = found
    pair = jnp.concatenate([up_ref[0:up_half], up_ref[up_half:value_rows]], axis=1)
    found = dot_nt(chosen, pair.reshape(up_half * LANES, slots)).reshape(
        micro, peers, up_half, LANES
    )
    if packed - down_half > up_half:
        rest = jnp.zeros((micro, peers, packed - down_half - up_half, LANES), F32)
        found = jnp.concatenate([found, rest], axis=2)
    panel_send[:, :, down_half:packed, :] = found.astype(BF16)

    pl.semaphore_wait(barrier, peers + 1)

    def spread(m, source, target, send_sem, recv_sem):
        def send(k, carry):
            peer = lax.rem(me + k, peers)
            pltpu.make_async_remote_copy(
                src_ref=source.at[m, peer],
                dst_ref=target.at[m, me],
                send_sem=send_sem.at[m],
                recv_sem=recv_sem.at[m],
                device_id={"dp": peer},
                device_id_type=pl.DeviceIdType.MESH,
            ).start()
            return carry

        pltpu.make_async_copy(source.at[m, me], target.at[m, me], recv_sem.at[m]).start()
        lax.fori_loop(1, peers, send, 0)

    def wait_for(ref, sem):
        pltpu.make_async_copy(ref, ref, sem).wait()

    for m in range(micro):
        spread(m, panel_send, panel_recv, panel_send_sem, panel_recv_sem)

    loads[2].wait()
    loads[3].wait()

    lane = lax.broadcasted_iota(jnp.int32, (CHUNK, LANES), 1)
    own_lanes = lane < LANES // 2

    def unpack(m):
        wait_for(panel_recv.at[m], panel_recv_sem.at[m])

        def one(source, carry):
            at = pl.multiple_of(source * feature_rows, 2 * GROUP)
            part = panel_recv[m, source, 0:down_half, :]
            panel_down[m, pl.ds(at, down_half), :] = part
            panel_down[m, pl.ds(at + down_half, down_half), :] = swap_halves(part)
            at = pl.multiple_of(source * value_rows, GROUP)
            part = panel_recv[m, source, down_half:packed, :].astype(F32)[0:up_half]
            both = jnp.concatenate([part, swap_halves(part)], axis=0)
            panel_up[m, pl.ds(at, value_rows), :] = both.astype(BF16)
            return carry

        lax.fori_loop(0, peers, one, 0)

    def forward(c):
        m = c // per_block
        here = chunk_rows(c)
        wait_for(h_in.at[here], h_recv_sem.at[c])
        total = jnp.zeros((CHUNK, 1), F32)
        for tile in tiles:
            hidden = h_in[here, tile].astype(F32)
            total += jnp.sum(hidden * hidden, axis=1, keepdims=True)
        factor = lax.rsqrt(total / width + EPSILON)
        inverse[here, :] = jnp.broadcast_to(factor, (CHUNK, LANES))
        mixed = jnp.zeros((CHUNK, w_value.shape[1]), F32)
        for tile in tiles:
            hidden = h_in[here, tile].astype(F32)
            part = (hidden * factor * gains[:, tile]).astype(BF16)
            normed[here, tile] = part
            mixed += dot(part, value_ref[tile, :])

        @pl.when(c % per_block == 0)
        def _():
            unpack(m)

        narrow = jnp.zeros((CHUNK, LANES), F32)
        for tile in tiles:
            narrow += dot(normed[here, tile], panel_down[m, tile, :])
        narrow = jnp.where(own_lanes, narrow, 0.0).astype(BF16)
        low[here, :] = narrow

        @pl.when(section < sections - 1)
        def _():
            values = (mixed + dot_nt(narrow, panel_up[m])).astype(BF16)
            for tile in tiles:
                added = dot(values, out_ref[:, tile])
                h_out[here, tile] = (h_in[here, tile].astype(F32) + added).astype(BF16)
            pltpu.make_async_remote_copy(
                src_ref=h_out.at[here],
                dst_ref=h_in.at[here],
                send_sem=h_send_sem.at[c],
                recv_sem=h_recv_sem.at[c],
                device_id={"section": section + 1},
                device_id_type=pl.DeviceIdType.MESH,
            ).start()

    def backward(c):
        m = c // per_block
        here = chunk_rows(c)
        wait_for(g_in.at[here], g_recv_sem.at[c])
        pulled = jnp.zeros((CHUNK, w_value.shape[1]), F32)
        for tile in tiles:
            pulled += dot_nt(g_in[here, tile], out_ref[:, tile])
        pulled = pulled.astype(BF16)
        value_grad[here, :] = pulled
        narrow = jnp.where(own_lanes, dot(pulled, panel_up[m]), 0.0).astype(BF16)
        low_grad[here, :] = narrow

        @pl.when(section > 0)
        def _():
            moment = jnp.zeros((CHUNK, 1), F32)
            for tile in tiles:
                part = dot_nt(pulled, value_ref[tile, :]) + dot_nt(narrow, panel_down[m, tile, :])
                part = part * gains[:, tile]
                scaled[:, tile] = part
                moment += jnp.sum(part * h_in[here, tile].astype(F32), axis=1, keepdims=True)
            factor = inverse[here, 0:1]
            bend = factor * factor * factor * (moment / width)
            for tile in tiles:
                result = (
                    g_in[here, tile].astype(F32)
                    + factor * scaled[:, tile]
                    - h_in[here, tile].astype(F32) * bend
                )
                g_out[here, tile] = result.astype(BF16)
            pltpu.make_async_remote_copy(
                src_ref=g_out.at[here],
                dst_ref=g_in.at[here],
                send_sem=g_send_sem.at[c],
                recv_sem=g_recv_sem.at[c],
                device_id={"section": section - 1},
                device_id_type=pl.DeviceIdType.MESH,
            ).start()

    def products(m):
        here = pl.ds(pl.multiple_of(m * block, block), block)
        for tile in tiles:
            product_down[tile, :] = dot_tn(normed[here, tile], low_grad[here, :]).astype(BF16)
        product_up[...] = dot_tn(value_grad[here, :], low[here, :])

        def pack(peer, carry):
            at = pl.multiple_of(peer * feature_rows, 2 * GROUP)
            part = product_down[pl.ds(at, down_half), :]
            other = product_down[pl.ds(at + down_half, down_half), :]
            grad_send[m, peer, 0:down_half, :] = part + swap_halves(other)
            at = pl.multiple_of(peer * value_rows, GROUP)
            part = product_up[pl.ds(at, value_rows), :]
            part = part[0:up_half] + swap_halves(part[up_half:value_rows])
            if packed - down_half > up_half:
                rest = jnp.zeros((packed - down_half - up_half, LANES), F32)
                part = jnp.concatenate([part, rest], axis=0)
            grad_send[m, peer, down_half:packed, :] = part.astype(BF16)
            return carry

        lax.fori_loop(0, peers, pack, 0)
        spread(m, grad_send, grad_recv, grad_send_sem, grad_recv_sem)

    lag = jnp.where(first, chunks, jnp.where(last, 0, (sections - 1 - section) * 3))
    lag = jnp.minimum(lag, chunks)

    def step(t, carry):
        @pl.when(t < chunks)
        def _():
            forward(t)

        c = t - lag

        @pl.when((c >= 0) & (c < chunks))
        def _():
            backward(c)

            @pl.when(c % per_block == per_block - 1)
            def _():
                products(c // per_block)

        return carry

    lax.fori_loop(0, chunks + lag, step, 0)

    for m in range(micro):
        wait_for(grad_recv.at[m], grad_recv_sem.at[m])
        for source, sem in ((panel_send, panel_send_sem), (grad_send, grad_send_sem)):
            wait_for(source.at[m, 0 : peers - 1], sem.at[m])

    @pl.when(section < sections - 1)
    def _():
        for c in range(chunks):
            wait_for(h_out.at[pl.ds(c * CHUNK, CHUNK)], h_send_sem.at[c])

    @pl.when(section > 0)
    def _():
        for c in range(chunks):
            wait_for(g_out.at[pl.ds(c * CHUNK, CHUNK)], g_send_sem.at[c])


def run_chain(tokens, cotangent, gains, w_value, w_out, down, up, criterion, slot_of):
    micro = criterion.shape[0]
    peers = lax.axis_size("dp")
    rows, width = tokens.shape
    value_width = w_out.shape[0]
    chunks = rows // CHUNK
    slots = down.shape[2]
    useful = (down.shape[0] + up.shape[0]) // 2
    packed = (useful + 15) // 16 * 16
    block = rows // micro
    spaces = [pl.BlockSpec(memory_space=pl.ANY)] * 2
    spaces += [pl.BlockSpec(memory_space=pltpu.VMEM)]
    spaces += [pl.BlockSpec(memory_space=pl.ANY)] * 4
    spaces += [pl.BlockSpec(memory_space=pltpu.SMEM)] * 2
    row_buffer = pltpu.VMEM((rows, width), BF16)
    exchange = (micro, peers, packed, LANES)
    return pl.pallas_call(
        chain_kernel,
        out_shape=jax.ShapeDtypeStruct(exchange, BF16),
        in_specs=spaces,
        out_specs=pl.BlockSpec(memory_space=pl.ANY),
        scratch_shapes=[
            pltpu.VMEM(w_value.shape, BF16),
            pltpu.VMEM(w_out.shape, BF16),
            pltpu.VMEM(down.shape, BF16),
            pltpu.VMEM(up.shape, BF16),
            pltpu.VMEM((micro * criterion.shape[1], slots), F32),
            row_buffer,
            row_buffer,
            row_buffer,
            row_buffer,
            row_buffer,
            pltpu.VMEM((rows, LANES), F32),
            pltpu.VMEM((rows, value_width), BF16),
            pltpu.VMEM((rows, LANES), BF16),
            pltpu.VMEM((rows, LANES), BF16),
            pltpu.VMEM((CHUNK, width), F32),
            pltpu.VMEM(exchange, BF16),
            pltpu.VMEM(exchange, BF16),
            pltpu.VMEM((micro, width, LANES), BF16),
            pltpu.VMEM((micro, value_width, LANES), BF16),
            pltpu.VMEM((width, LANES), BF16),
            pltpu.VMEM((value_width, LANES), F32),
            pltpu.VMEM(exchange, BF16),
            pltpu.SemaphoreType.DMA((4,)),
            pltpu.SemaphoreType.DMA((chunks,)),
            pltpu.SemaphoreType.DMA((chunks,)),
            pltpu.SemaphoreType.DMA((chunks,)),
            pltpu.SemaphoreType.DMA((chunks,)),
            pltpu.SemaphoreType.DMA((micro,)),
            pltpu.SemaphoreType.DMA((micro,)),
            pltpu.SemaphoreType.DMA((micro,)),
            pltpu.SemaphoreType.DMA((micro,)),
        ],
        compiler_params=pltpu.CompilerParams(
            collective_id=0, has_side_effects=True, vmem_limit_bytes=56 * 1024 * 1024
        ),
        name="chain",
    )(tokens, cotangent, gains, w_value, w_out, down, up, criterion, slot_of)


def place_kernel(criterion, slot_of, parts, down, up, picks):
    step = pl.program_id(0)
    pairs = parts.shape[0]
    up_half = up.shape[0] // 2

    @pl.when(step == 0)
    def _():
        fill_picks(picks, criterion, slot_of)

    chosen = picks[...].astype(BF16)
    flat = parts[...].reshape(pairs, GROUP * LANES)
    summed = dot_tn(flat, chosen).reshape(GROUP, 2, LANES // 2, picks.shape[1])

    @pl.when(step < pl.num_programs(0) - 1)
    def _():
        down[0] = summed[:, 0]
        down[1] = summed[:, 1]

    @pl.when(step == pl.num_programs(0) - 1)
    def _():
        up[0:up_half] = summed[0:up_half, 0]
        up[up_half : 2 * up_half] = summed[0:up_half, 1]


def place(criterion, slot_of, parts, feature_rows, value_rows, slots, rank):
    pairs = parts.shape[0]
    down_half = feature_rows // 2
    steps = down_half // GROUP
    down, up = pl.pallas_call(
        place_kernel,
        grid=(steps + 1,),
        in_specs=[
            pl.BlockSpec(memory_space=pltpu.SMEM),
            pl.BlockSpec(memory_space=pltpu.SMEM),
            pl.BlockSpec((pairs, GROUP, LANES), lambda i: (0, i, 0)),
        ],
        out_specs=[
            pl.BlockSpec((2, GROUP, rank, slots), lambda i: (0, jnp.minimum(i, steps - 1), 0, 0)),
            pl.BlockSpec((value_rows, rank, slots), lambda i: (0, 0, 0)),
        ],
        out_shape=[
            jax.ShapeDtypeStruct((2, down_half, rank, slots), F32),
            jax.ShapeDtypeStruct((value_rows, rank, slots), F32),
        ],
        scratch_shapes=[pltpu.VMEM((pairs, slots), F32)],
        compiler_params=pltpu.CompilerParams(vmem_limit_bytes=32 * 1024 * 1024),
        name="place",
    )(criterion, slot_of, parts)
    return down.reshape(feature_rows, rank, slots), up


def on_device(
    tokens,
    cotangent,
    norm_gain,
    value_weight,
    out_weight,
    adapter_down,
    adapter_up,
    criterion,
    slot_of,
):
    micro, block, width = tokens.shape
    down = jnp.transpose(adapter_down[0], (1, 2, 0))
    up = jnp.transpose(adapter_up[0], (1, 2, 0))
    parts = run_chain(
        tokens.reshape(micro * block, width),
        cotangent.reshape(micro * block, width),
        norm_gain,
        value_weight[0],
        out_weight[0],
        down,
        up,
        criterion,
        slot_of,
    )
    parts = parts.reshape((parts.shape[0] * parts.shape[1],) + parts.shape[2:])
    grad_down, grad_up = place(
        criterion, slot_of, parts, down.shape[0], up.shape[0], down.shape[2], down.shape[1]
    )
    return (jnp.transpose(grad_down, (2, 0, 1))[None], jnp.transpose(grad_up, (2, 0, 1))[None])


def solution(mesh):
    return jax.shard_map(
        on_device,
        mesh=mesh,
        in_specs=(
            P(None, "dp", None),
            P(None, "dp", None),
            P("section", None),
            P("section", None, None),
            P("section", None, None),
            P("section", None, "dp", None),
            P("section", None, "dp", None),
            P(),
            P(),
        ),
        out_specs=(P("section", None, "dp", None), P("section", None, "dp", None)),
        check_vma=False,
    )
```

```python
import jax
import jax.numpy as jnp
from jax import lax
from jax.experimental import pallas as pl
from jax.experimental.pallas import tpu as pltpu
from jax.sharding import PartitionSpec as P

EPSILON = 1e-06
CHUNK = 32
TILE = 512
GROUP = 16
PIECES = 2
LANES = 128
BF16 = jnp.bfloat16
F32 = jnp.float32


def dot(left, right):
    return jnp.dot(left, right, preferred_element_type=F32)


def dot_nt(left, right):
    return lax.dot_general(left, right, (((1,), (1,)), ((), ())), preferred_element_type=F32)


def dot_tn(left, right):
    return lax.dot_general(left, right, (((0,), (0,)), ((), ())), preferred_element_type=F32)


def swap_halves(value):
    half = value.shape[-1] // 2
    return jnp.concatenate([value[:, half:], value[:, :half]], axis=1)


def fill_picks(picks, criterion, slot_of):
    micro, blocks = criterion.shape
    lanes = lax.broadcasted_iota(jnp.int32, (1, picks.shape[1]), 1)
    for index in range(micro * blocks):
        slot = slot_of[criterion[index // blocks, index % blocks]]
        picks[index : index + 1, :] = jnp.where(lanes == slot, 1.0, 0.0)


def chain_kernel(
    tokens,
    cotangent,
    gains,
    w_value,
    w_out,
    down,
    up,
    criterion,
    slot_of,
    grad_recv,
    value_ref,
    out_ref,
    value_turned,
    out_turned,
    down_ref,
    up_ref,
    picks,
    h_in,
    h_out,
    g_in,
    g_out,
    scaled,
    inverse,
    mixed_ref,
    narrow_ref,
    value_grad,
    low,
    low_grad,
    panel_send,
    panel_recv,
    panel_down,
    panel_up,
    product_down,
    product_up,
    grad_send,
    load_sem,
    h_send_sem,
    h_recv_sem,
    g_send_sem,
    g_recv_sem,
    panel_send_sem,
    panel_recv_sem,
    grad_send_sem,
    grad_recv_sem,
):
    sections = lax.axis_size("section")
    peers = lax.axis_size("dp")
    section = lax.axis_index("section")
    me = lax.axis_index("dp")
    micro = criterion.shape[0]
    rows, width = h_in.shape
    block = rows // micro
    chunks = rows // CHUNK
    per_block = block // CHUNK
    slots = picks.shape[1]
    feature_rows = down.shape[0]
    value_rows = up.shape[0]
    down_half = feature_rows // 2
    up_half = value_rows // 2
    packed = panel_send.shape[2]
    value_width = value_grad.shape[1]
    piece_width = width // PIECES
    pieces = [slice(start, start + piece_width) for start in range(0, width, piece_width)]
    first = section == 0
    last = section == sections - 1

    loads = [
        pltpu.make_async_copy(source, target, load_sem.at[place])
        for place, (source, target) in enumerate(
            [(down, down_ref), (up, up_ref), (w_value, value_ref), (w_out, out_ref)]
        )
    ]
    for load in loads:
        load.start()

    def tiles_of(piece):
        base = piece * piece_width
        return [slice(base + at, base + at + TILE) for at in range(0, piece_width, TILE)]

    def chunk_rows(c):
        return pl.ds(pl.multiple_of(c * CHUNK, CHUNK), CHUNK)

    @pl.when(first)
    def _():
        for c in range(chunks):
            part = pl.ds(c * CHUNK, CHUNK)
            for piece in range(PIECES):
                pltpu.make_async_copy(
                    tokens.at[part, pieces[piece]],
                    h_in.at[part, pieces[piece]],
                    h_recv_sem.at[c, piece],
                ).start()

    @pl.when(last)
    def _():
        for c in range(chunks):
            part = pl.ds(c * CHUNK, CHUNK)
            for piece in range(PIECES):
                pltpu.make_async_copy(
                    cotangent.at[part, pieces[piece]],
                    g_in.at[part, pieces[piece]],
                    g_recv_sem.at[c, piece],
                ).start()

    barrier = pltpu.get_barrier_semaphore()

    def greet(k, carry):
        pl.semaphore_signal(
            barrier,
            inc=1,
            device_id={"dp": lax.rem(me + k, peers)},
            device_id_type=pl.DeviceIdType.MESH,
        )
        return carry

    lax.fori_loop(1, peers, greet, 0)
    for step in (1, sections - 1):
        pl.semaphore_signal(
            barrier,
            inc=1,
            device_id={"section": lax.rem(section + step, sections)},
            device_id_type=pl.DeviceIdType.MESH,
        )

    fill_picks(picks, criterion, slot_of)
    chosen = picks[...].astype(BF16)
    loads[0].wait()
    loads[1].wait()
    for start in range(0, down_half, GROUP):
        pair = jnp.concatenate(
            [down_ref[start : start + GROUP], down_ref[down_half + start : down_half + start + GROUP]],
            axis=1,
        )
        found = dot_nt(chosen, pair.reshape(GROUP * LANES, slots))
        found = found.reshape(micro, peers, GROUP, LANES).astype(BF16)
        panel_send[:, :, start : start + GROUP, :] = found
    pair = jnp.concatenate([up_ref[0:up_half], up_ref[up_half:value_rows]], axis=1)
    found = dot_nt(chosen, pair.reshape(up_half * LANES, slots)).reshape(
        micro, peers, up_half, LANES
    )
    if packed - down_half > up_half:
        rest = jnp.zeros((micro, peers, packed - down_half - up_half, LANES), F32)
        found = jnp.concatenate([found, rest], axis=2)
    panel_send[:, :, down_half:packed, :] = found.astype(BF16)

    pl.semaphore_wait(barrier, peers + 1)

    def spread(m, source, target, send_sem, recv_sem):
        def send(k, carry):
            peer = lax.rem(me + k, peers)
            pltpu.make_async_remote_copy(
                src_ref=source.at[m, peer],
                dst_ref=target.at[m, me],
                send_sem=send_sem.at[m],
                recv_sem=recv_sem.at[m],
                device_id={"dp": peer},
                device_id_type=pl.DeviceIdType.MESH,
            ).start()
            return carry

        pltpu.make_async_copy(source.at[m, me], target.at[m, me], recv_sem.at[m]).start()
        lax.fori_loop(1, peers, send, 0)

    def wait_for(ref, sem):
        pltpu.make_async_copy(ref, ref, sem).wait()

    for m in range(micro):
        spread(m, panel_send, panel_recv, panel_send_sem, panel_recv_sem)

    loads[2].wait()
    loads[3].wait()

    def unpack(m):
        wait_for(panel_recv.at[m], panel_recv_sem.at[m])
        near = lax.broadcasted_iota(jnp.int32, (down_half, LANES), 1) < LANES // 2
        near_up = lax.broadcasted_iota(jnp.int32, (up_half, LANES), 1) < LANES // 2

        def one(source, carry):
            at = pl.multiple_of(source * feature_rows, 2 * GROUP)
            part = panel_recv[m, source, 0:down_half, :]
            none = jnp.zeros_like(part)
            panel_down[m, pl.ds(at, down_half), :] = jnp.where(near, part, none)
            panel_down[m, pl.ds(at + down_half, down_half), :] = jnp.where(near, none, part)
            at = pl.multiple_of(source * value_rows, GROUP)
            part = panel_recv[m, source, down_half:packed, :].astype(F32)[0:up_half]
            both = [jnp.where(near_up, part, 0.0), jnp.where(near_up, 0.0, part)]
            panel_up[m, pl.ds(at, value_rows), :] = jnp.concatenate(both, axis=0).astype(BF16)
            return carry

        lax.fori_loop(0, peers, one, 0)

    def send_piece(source, target, c, piece, send_sem, recv_sem, to):
        here = chunk_rows(c)
        columns = pieces[piece]
        pltpu.make_async_remote_copy(
            src_ref=source.at[here, columns],
            dst_ref=target.at[here, columns],
            send_sem=send_sem.at[c, piece],
            recv_sem=recv_sem.at[c, piece],
            device_id={"section": to},
            device_id_type=pl.DeviceIdType.MESH,
        ).start()

    def forward(c):
        m = c // per_block
        here = chunk_rows(c)
        squares = jnp.zeros((CHUNK, LANES), F32)
        mixed = jnp.zeros((CHUNK, value_width), F32)
        for piece in range(PIECES):
            wait_for(h_in.at[here, pieces[piece]], h_recv_sem.at[c, piece])
            for tile in tiles_of(piece):
                hidden = h_in[here, tile].astype(F32)
                square = hidden * hidden
                for start in range(0, TILE, LANES):
                    squares += square[:, start : start + LANES]
                part = (hidden * gains[:, tile]).astype(BF16)
                scaled[here, tile] = part
                mixed += dot(part, value_ref[tile, :])
        total = jnp.sum(squares, axis=1, keepdims=True)
        factor = lax.rsqrt(total / width + EPSILON)
        inverse[here, :] = jnp.broadcast_to(factor, (CHUNK, LANES))
        mixed_ref[here, :] = mixed

        @pl.when(c % per_block == 0)
        def _():
            unpack(m)

        narrow = jnp.zeros((CHUNK, LANES), F32)
        for piece in range(PIECES):
            for tile in tiles_of(piece):
                narrow += dot(scaled[here, tile], panel_down[m, tile, :])
        narrow_ref[here, :] = narrow
        narrow = ((narrow + swap_halves(narrow)) * factor).astype(BF16)
        low[here, :] = narrow

        @pl.when(section < sections - 1)
        def _():
            values = (mixed * factor + dot_nt(narrow, panel_up[m])).astype(BF16)
            for piece in range(PIECES):
                for tile in tiles_of(piece):
                    added = dot(values, out_ref[:, tile])
                    h_out[here, tile] = (h_in[here, tile].astype(F32) + added).astype(BF16)
                send_piece(h_out, h_in, c, piece, h_send_sem, h_recv_sem, section + 1)

    def backward(c):
        m = c // per_block
        here = chunk_rows(c)
        pulled = jnp.zeros((CHUNK, value_width), F32)
        for piece in range(PIECES):
            wait_for(g_in.at[here, pieces[piece]], g_recv_sem.at[c, piece])
            for tile in tiles_of(piece):
                pulled += dot(g_in[here, tile], out_turned[tile, :])
        pulled = pulled.astype(BF16)
        value_grad[here, :] = pulled
        narrow = dot(pulled, panel_up[m])
        narrow = narrow + swap_halves(narrow)
        factor = inverse[here, 0:1]
        low_grad[here, :] = (narrow * factor).astype(BF16)

        @pl.when(section > 0)
        def _():
            held = narrow.astype(BF16)
            along = pulled.astype(F32) * mixed_ref[here, :]
            moment = jnp.sum(along, axis=1, keepdims=True)
            along = held.astype(F32) * narrow_ref[here, :]
            moment += jnp.sum(along, axis=1, keepdims=True)
            bend = factor * factor * factor * (moment / width)
            for piece in range(PIECES):
                for tile in tiles_of(piece):
                    part = dot(pulled, value_turned[:, tile])
                    part += dot_nt(held, panel_down[m, tile, :])
                    result = (
                        g_in[here, tile].astype(F32)
                        + factor * (part * gains[:, tile])
                        - h_in[here, tile].astype(F32) * bend
                    )
                    g_out[here, tile] = result.astype(BF16)
                send_piece(g_out, g_in, c, piece, g_send_sem, g_recv_sem, section - 1)

    def products(m):
        here = pl.ds(pl.multiple_of(m * block, block), block)
        for start in range(0, width, TILE):
            tile = slice(start, start + TILE)
            product_down[tile, :] = dot_tn(scaled[here, tile], low_grad[here, :]).astype(BF16)
        product_up[...] = dot_tn(value_grad[here, :], low[here, :])
        near = lax.broadcasted_iota(jnp.int32, (down_half, LANES), 1) < LANES // 2
        near_up = lax.broadcasted_iota(jnp.int32, (up_half, LANES), 1) < LANES // 2

        def pack(peer, carry):
            at = pl.multiple_of(peer * feature_rows, 2 * GROUP)
            part = product_down[pl.ds(at, down_half), :]
            other = product_down[pl.ds(at + down_half, down_half), :]
            grad_send[m, peer, 0:down_half, :] = jnp.where(near, part, other)
            at = pl.multiple_of(peer * value_rows, GROUP)
            part = product_up[pl.ds(at, value_rows), :]
            part = jnp.where(near_up, part[0:up_half], part[up_half:value_rows])
            if packed - down_half > up_half:
                rest = jnp.zeros((packed - down_half - up_half, LANES), F32)
                part = jnp.concatenate([part, rest], axis=0)
            grad_send[m, peer, down_half:packed, :] = part.astype(BF16)
            return carry

        lax.fori_loop(0, peers, pack, 0)
        spread(m, grad_send, grad_recv, grad_send_sem, grad_recv_sem)

    def turn():
        def one(index, carry):
            at = pl.ds(pl.multiple_of(index * TILE, TILE), TILE)
            out_turned[at, :] = out_ref[:, at].T
            value_turned[:, at] = value_ref[at, :].T
            return carry

        lax.fori_loop(0, width // TILE, one, 0)

    lag = jnp.where(first, chunks, jnp.where(last, 0, (sections - 1 - section) * 3))
    lag = jnp.minimum(lag, chunks)

    turn_at = jnp.where(first, chunks, 0)

    def step(t, carry):
        @pl.when(t == turn_at)
        def _():
            turn()

        @pl.when(t < chunks)
        def _():
            forward(t)

        c = t - lag

        @pl.when((c >= 0) & (c < chunks))
        def _():
            backward(c)

            @pl.when(c % per_block == per_block - 1)
            def _():
                products(c // per_block)

        return carry

    lax.fori_loop(0, chunks + lag, step, 0)

    for m in range(micro):
        wait_for(grad_recv.at[m], grad_recv_sem.at[m])
        for source, sem in ((panel_send, panel_send_sem), (grad_send, grad_send_sem)):
            wait_for(source.at[m, 0 : peers - 1], sem.at[m])

    @pl.when(section < sections - 1)
    def _():
        for c in range(chunks):
            for piece in range(PIECES):
                part = h_out.at[pl.ds(c * CHUNK, CHUNK), pieces[piece]]
                wait_for(part, h_send_sem.at[c, piece])

    @pl.when(section > 0)
    def _():
        for c in range(chunks):
            for piece in range(PIECES):
                part = g_out.at[pl.ds(c * CHUNK, CHUNK), pieces[piece]]
                wait_for(part, g_send_sem.at[c, piece])


def run_chain(tokens, cotangent, gains, w_value, w_out, down, up, criterion, slot_of):
    micro = criterion.shape[0]
    peers = lax.axis_size("dp")
    rows, width = tokens.shape
    value_width = w_out.shape[0]
    chunks = rows // CHUNK
    slots = down.shape[2]
    useful = (down.shape[0] + up.shape[0]) // 2
    packed = (useful + 15) // 16 * 16
    block = rows // micro
    spaces = [pl.BlockSpec(memory_space=pl.ANY)] * 2
    spaces += [pl.BlockSpec(memory_space=pltpu.VMEM)]
    spaces += [pl.BlockSpec(memory_space=pl.ANY)] * 4
    spaces += [pl.BlockSpec(memory_space=pltpu.SMEM)] * 2
    row_buffer = pltpu.VMEM((rows, width), BF16)
    exchange = (micro, peers, packed, LANES)
    return pl.pallas_call(
        chain_kernel,
        out_shape=jax.ShapeDtypeStruct(exchange, BF16),
        in_specs=spaces,
        out_specs=pl.BlockSpec(memory_space=pl.ANY),
        scratch_shapes=[
            pltpu.VMEM(w_value.shape, BF16),
            pltpu.VMEM(w_out.shape, BF16),
            pltpu.VMEM(w_out.shape, BF16),
            pltpu.VMEM(w_value.shape, BF16),
            pltpu.VMEM(down.shape, BF16),
            pltpu.VMEM(up.shape, BF16),
            pltpu.VMEM((micro * criterion.shape[1], slots), F32),
            row_buffer,
            row_buffer,
            row_buffer,
            row_buffer,
            row_buffer,
            pltpu.VMEM((rows, LANES), F32),
            pltpu.VMEM((rows, value_width), F32),
            pltpu.VMEM((rows, LANES), F32),
            pltpu.VMEM((rows, value_width), BF16),
            pltpu.VMEM((rows, LANES), BF16),
            pltpu.VMEM((rows, LANES), BF16),
            pltpu.VMEM(exchange, BF16),
            pltpu.VMEM(exchange, BF16),
            pltpu.VMEM((micro, width, LANES), BF16),
            pltpu.VMEM((micro, value_width, LANES), BF16),
            pltpu.VMEM((width, LANES), BF16),
            pltpu.VMEM((value_width, LANES), F32),
            pltpu.VMEM(exchange, BF16),
            pltpu.SemaphoreType.DMA((4,)),
            pltpu.SemaphoreType.DMA((chunks, PIECES)),
            pltpu.SemaphoreType.DMA((chunks, PIECES)),
            pltpu.SemaphoreType.DMA((chunks, PIECES)),
            pltpu.SemaphoreType.DMA((chunks, PIECES)),
            pltpu.SemaphoreType.DMA((micro,)),
            pltpu.SemaphoreType.DMA((micro,)),
            pltpu.SemaphoreType.DMA((micro,)),
            pltpu.SemaphoreType.DMA((micro,)),
        ],
        compiler_params=pltpu.CompilerParams(
            collective_id=0, has_side_effects=True, vmem_limit_bytes=56 * 1024 * 1024
        ),
        name="chain",
    )(tokens, cotangent, gains, w_value, w_out, down, up, criterion, slot_of)


def place_kernel(criterion, slot_of, parts, down, up, picks):
    step = pl.program_id(0)
    pairs = parts.shape[0]
    up_half = up.shape[0] // 2

    @pl.when(step == 0)
    def _():
        fill_picks(picks, criterion, slot_of)

    chosen = picks[...].astype(BF16)
    flat = parts[...].reshape(pairs, GROUP * LANES)
    summed = dot_tn(flat, chosen).reshape(GROUP, 2, LANES // 2, picks.shape[1])

    @pl.when(step < pl.num_programs(0) - 1)
    def _():
        down[0] = summed[:, 0]
        down[1] = summed[:, 1]

    @pl.when(step == pl.num_programs(0) - 1)
    def _():
        up[0:up_half] = summed[0:up_half, 0]
        up[up_half : 2 * up_half] = summed[0:up_half, 1]


def place(criterion, slot_of, parts, feature_rows, value_rows, slots, rank):
    pairs = parts.shape[0]
    down_half = feature_rows // 2
    steps = down_half // GROUP
    down, up = pl.pallas_call(
        place_kernel,
        grid=(steps + 1,),
        in_specs=[
            pl.BlockSpec(memory_space=pltpu.SMEM),
            pl.BlockSpec(memory_space=pltpu.SMEM),
            pl.BlockSpec((pairs, GROUP, LANES), lambda i: (0, i, 0)),
        ],
        out_specs=[
            pl.BlockSpec((2, GROUP, rank, slots), lambda i: (0, jnp.minimum(i, steps - 1), 0, 0)),
            pl.BlockSpec((value_rows, rank, slots), lambda i: (0, 0, 0)),
        ],
        out_shape=[
            jax.ShapeDtypeStruct((2, down_half, rank, slots), F32),
            jax.ShapeDtypeStruct((value_rows, rank, slots), F32),
        ],
        scratch_shapes=[pltpu.VMEM((pairs, slots), F32)],
        compiler_params=pltpu.CompilerParams(vmem_limit_bytes=32 * 1024 * 1024),
        name="place",
    )(criterion, slot_of, parts)
    return down.reshape(feature_rows, rank, slots), up


def on_device(
    tokens,
    cotangent,
    norm_gain,
    value_weight,
    out_weight,
    adapter_down,
    adapter_up,
    criterion,
    slot_of,
):
    micro, block, width = tokens.shape
    down = jnp.transpose(adapter_down[0], (1, 2, 0))
    up = jnp.transpose(adapter_up[0], (1, 2, 0))
    parts = run_chain(
        tokens.reshape(micro * block, width),
        cotangent.reshape(micro * block, width),
        norm_gain,
        value_weight[0],
        out_weight[0],
        down,
        up,
        criterion,
        slot_of,
    )
    parts = parts.reshape((parts.shape[0] * parts.shape[1],) + parts.shape[2:])
    grad_down, grad_up = place(
        criterion, slot_of, parts, down.shape[0], up.shape[0], down.shape[2], down.shape[1]
    )
    return (jnp.transpose(grad_down, (2, 0, 1))[None], jnp.transpose(grad_up, (2, 0, 1))[None])


def solution(mesh):
    return jax.shard_map(
        on_device,
        mesh=mesh,
        in_specs=(
            P(None, "dp", None),
            P(None, "dp", None),
            P("section", None),
            P("section", None, None),
            P("section", None, None),
            P("section", None, "dp", None),
            P("section", None, "dp", None),
            P(),
            P(),
        ),
        out_specs=(P("section", None, "dp", None), P("section", None, "dp", None)),
        check_vma=False,
    )
```

```python
import jax
import jax.numpy as jnp
from jax import lax
from jax.experimental import pallas as pl
from jax.experimental.pallas import tpu as pltpu
from jax.sharding import PartitionSpec as P

EPSILON = 1e-06
CHUNK = 16
TILE = 512
GROUP = 16
PIECES = 2
LANES = 128
BF16 = jnp.bfloat16
F32 = jnp.float32


def dot(left, right):
    return jnp.dot(left, right, preferred_element_type=F32)


def dot_nt(left, right):
    return lax.dot_general(left, right, (((1,), (1,)), ((), ())), preferred_element_type=F32)


def dot_tn(left, right):
    return lax.dot_general(left, right, (((0,), (0,)), ((), ())), preferred_element_type=F32)


def swap_halves(value):
    half = value.shape[-1] // 2
    return jnp.concatenate([value[:, half:], value[:, :half]], axis=1)


def fill_picks(picks, criterion, slot_of):
    micro, blocks = criterion.shape
    lanes = lax.broadcasted_iota(jnp.int32, (1, picks.shape[1]), 1)
    for index in range(micro * blocks):
        slot = slot_of[criterion[index // blocks, index % blocks]]
        picks[index : index + 1, :] = jnp.where(lanes == slot, 1.0, 0.0)


def chain_kernel(
    tokens,
    cotangent,
    gains,
    w_value,
    w_out,
    down,
    up,
    criterion,
    slot_of,
    grad_recv,
    value_ref,
    out_ref,
    value_turned,
    out_turned,
    down_ref,
    up_ref,
    picks,
    h_in,
    h_out,
    g_in,
    g_out,
    scaled,
    inverse,
    mixed_ref,
    narrow_ref,
    value_grad,
    low,
    low_grad,
    panel_send,
    panel_recv,
    panel_down,
    panel_up,
    product_down,
    product_up,
    grad_send,
    load_sem,
    h_send_sem,
    h_recv_sem,
    g_send_sem,
    g_recv_sem,
    panel_send_sem,
    panel_recv_sem,
    grad_send_sem,
    grad_recv_sem,
):
    sections = lax.axis_size("section")
    peers = lax.axis_size("dp")
    section = lax.axis_index("section")
    me = lax.axis_index("dp")
    micro = criterion.shape[0]
    rows, width = h_in.shape
    block = rows // micro
    chunks = rows // CHUNK
    per_block = block // CHUNK
    slots = picks.shape[1]
    feature_rows = down.shape[0]
    value_rows = up.shape[0]
    down_half = feature_rows // 2
    up_half = value_rows // 2
    packed = panel_send.shape[2]
    value_width = value_grad.shape[1]
    piece_width = width // PIECES
    pieces = [slice(start, start + piece_width) for start in range(0, width, piece_width)]
    first = section == 0
    last = section == sections - 1

    loads = [
        pltpu.make_async_copy(source, target, load_sem.at[place])
        for place, (source, target) in enumerate(
            [(down, down_ref), (up, up_ref), (w_value, value_ref), (w_out, out_ref)]
        )
    ]
    loads[0].start()
    loads[1].start()

    def tiles_of(piece):
        base = piece * piece_width
        return [slice(base + at, base + at + TILE) for at in range(0, piece_width, TILE)]

    def chunk_rows(c):
        return pl.ds(pl.multiple_of(c * CHUNK, CHUNK), CHUNK)

    barrier = pltpu.get_barrier_semaphore()

    def greet(k, carry):
        pl.semaphore_signal(
            barrier,
            inc=1,
            device_id={"dp": lax.rem(me + k, peers)},
            device_id_type=pl.DeviceIdType.MESH,
        )
        return carry

    lax.fori_loop(1, peers, greet, 0)
    for step in (1, sections - 1):
        pl.semaphore_signal(
            barrier,
            inc=1,
            device_id={"section": lax.rem(section + step, sections)},
            device_id_type=pl.DeviceIdType.MESH,
        )

    fill_picks(picks, criterion, slot_of)
    chosen = picks[...].astype(BF16)
    loads[0].wait()
    loads[1].wait()
    loads[2].start()

    @pl.when(first)
    def _():
        for c in range(chunks):
            part = pl.ds(c * CHUNK, CHUNK)
            for piece in range(PIECES):
                pltpu.make_async_copy(
                    tokens.at[part, pieces[piece]],
                    h_in.at[part, pieces[piece]],
                    h_recv_sem.at[c, piece],
                ).start()

    @pl.when(last)
    def _():
        for c in range(chunks):
            part = pl.ds(c * CHUNK, CHUNK)
            for piece in range(PIECES):
                pltpu.make_async_copy(
                    cotangent.at[part, pieces[piece]],
                    g_in.at[part, pieces[piece]],
                    g_recv_sem.at[c, piece],
                ).start()

    loads[3].start()
    for start in range(0, down_half, GROUP):
        pair = jnp.concatenate(
            [down_ref[start : start + GROUP], down_ref[down_half + start : down_half + start + GROUP]],
            axis=1,
        )
        found = dot_nt(chosen, pair.reshape(GROUP * LANES, slots))
        found = found.reshape(micro, peers, GROUP, LANES).astype(BF16)
        panel_send[:, :, start : start + GROUP, :] = found
    pair = jnp.concatenate([up_ref[0:up_half], up_ref[up_half:value_rows]], axis=1)
    found = dot_nt(chosen, pair.reshape(up_half * LANES, slots)).reshape(
        micro, peers, up_half, LANES
    )
    if packed - down_half > up_half:
        rest = jnp.zeros((micro, peers, packed - down_half - up_half, LANES), F32)
        found = jnp.concatenate([found, rest], axis=2)
    panel_send[:, :, down_half:packed, :] = found.astype(BF16)

    pl.semaphore_wait(barrier, peers + 1)

    def spread(m, source, target, send_sem, recv_sem):
        def send(k, carry):
            peer = lax.rem(me + k, peers)
            pltpu.make_async_remote_copy(
                src_ref=source.at[m, peer],
                dst_ref=target.at[m, me],
                send_sem=send_sem.at[m],
                recv_sem=recv_sem.at[m],
                device_id={"dp": peer},
                device_id_type=pl.DeviceIdType.MESH,
            ).start()
            return carry

        pltpu.make_async_copy(source.at[m, me], target.at[m, me], recv_sem.at[m]).start()
        lax.fori_loop(1, peers, send, 0)

    def wait_for(ref, sem):
        pltpu.make_async_copy(ref, ref, sem).wait()

    for m in range(micro):
        spread(m, panel_send, panel_recv, panel_send_sem, panel_recv_sem)

    loads[2].wait()

    def unpack(m):
        wait_for(panel_recv.at[m], panel_recv_sem.at[m])
        near = lax.broadcasted_iota(jnp.int32, (down_half, LANES), 1) < LANES // 2
        near_up = lax.broadcasted_iota(jnp.int32, (up_half, LANES), 1) < LANES // 2

        def one(source, carry):
            at = pl.multiple_of(source * feature_rows, 2 * GROUP)
            part = panel_recv[m, source, 0:down_half, :]
            none = jnp.zeros_like(part)
            panel_down[m, pl.ds(at, down_half), :] = jnp.where(near, part, none)
            panel_down[m, pl.ds(at + down_half, down_half), :] = jnp.where(near, none, part)
            at = pl.multiple_of(source * value_rows, GROUP)
            part = panel_recv[m, source, down_half:packed, :].astype(F32)[0:up_half]
            both = [jnp.where(near_up, part, 0.0), jnp.where(near_up, 0.0, part)]
            panel_up[m, pl.ds(at, value_rows), :] = jnp.concatenate(both, axis=0).astype(BF16)
            return carry

        lax.fori_loop(0, peers, one, 0)

    def send_piece(source, target, c, piece, send_sem, recv_sem, to):
        here = chunk_rows(c)
        columns = pieces[piece]
        pltpu.make_async_remote_copy(
            src_ref=source.at[here, columns],
            dst_ref=target.at[here, columns],
            send_sem=send_sem.at[c, piece],
            recv_sem=recv_sem.at[c, piece],
            device_id={"section": to},
            device_id_type=pl.DeviceIdType.MESH,
        ).start()

    def forward(c):
        m = c // per_block
        here = chunk_rows(c)
        squares = jnp.zeros((CHUNK, LANES), F32)
        mixed = jnp.zeros((CHUNK, value_width), F32)
        for piece in range(PIECES):
            wait_for(h_in.at[here, pieces[piece]], h_recv_sem.at[c, piece])
            for tile in tiles_of(piece):
                hidden = h_in[here, tile].astype(F32)
                square = hidden * hidden
                for start in range(0, TILE, LANES):
                    squares += square[:, start : start + LANES]
                part = (hidden * gains[:, tile]).astype(BF16)
                scaled[here, tile] = part
                mixed += dot(part, value_ref[tile, :])
        total = jnp.sum(squares, axis=1, keepdims=True)
        factor = lax.rsqrt(total / width + EPSILON)
        inverse[here, :] = jnp.broadcast_to(factor, (CHUNK, LANES))
        mixed_ref[here, :] = mixed

        @pl.when(first & (c % per_block == 0))
        def _():
            unpack(m)

        narrow = jnp.zeros((CHUNK, LANES), F32)
        for piece in range(PIECES):
            for tile in tiles_of(piece):
                narrow += dot(scaled[here, tile], panel_down[m, tile, :])
        narrow_ref[here, :] = narrow
        narrow = ((narrow + swap_halves(narrow)) * factor).astype(BF16)
        low[here, :] = narrow

        @pl.when(section < sections - 1)
        def _():
            values = (mixed * factor + dot_nt(narrow, panel_up[m])).astype(BF16)
            for piece in range(PIECES):
                for tile in tiles_of(piece):
                    added = dot(values, out_ref[:, tile])
                    h_out[here, tile] = (h_in[here, tile].astype(F32) + added).astype(BF16)
                send_piece(h_out, h_in, c, piece, h_send_sem, h_recv_sem, section + 1)

    def pull(c, carry):
        here = chunk_rows(c)
        pulled = jnp.zeros((CHUNK, value_width), F32)
        for piece in range(PIECES):
            wait_for(g_in.at[here, pieces[piece]], g_recv_sem.at[c, piece])
            for tile in tiles_of(piece):
                pulled += dot(g_in[here, tile], out_turned[tile, :])
        value_grad[here, :] = pulled.astype(BF16)
        return carry

    def backward(c):
        m = c // per_block
        here = chunk_rows(c)
        pulled = value_grad[here, :]
        narrow = dot(pulled, panel_up[m])
        narrow = narrow + swap_halves(narrow)
        factor = inverse[here, 0:1]
        low_grad[here, :] = (narrow * factor).astype(BF16)

        @pl.when(section > 0)
        def _():
            held = narrow.astype(BF16)
            along = pulled.astype(F32) * mixed_ref[here, :]
            moment = jnp.sum(along, axis=1, keepdims=True)
            along = held.astype(F32) * narrow_ref[here, :]
            moment += jnp.sum(along, axis=1, keepdims=True)
            bend = factor * factor * factor * (moment / width)
            for piece in range(PIECES):
                for tile in tiles_of(piece):
                    part = dot(pulled, value_turned[:, tile])
                    part += dot_nt(held, panel_down[m, tile, :])
                    result = (
                        g_in[here, tile].astype(F32)
                        + factor * (part * gains[:, tile])
                        - h_in[here, tile].astype(F32) * bend
                    )
                    g_out[here, tile] = result.astype(BF16)
                send_piece(g_out, g_in, c, piece, g_send_sem, g_recv_sem, section - 1)

    def products(m):
        here = pl.ds(pl.multiple_of(m * block, block), block)
        for start in range(0, width, TILE):
            tile = slice(start, start + TILE)
            product_down[tile, :] = dot_tn(scaled[here, tile], low_grad[here, :]).astype(BF16)
        product_up[...] = dot_tn(value_grad[here, :], low[here, :])
        near = lax.broadcasted_iota(jnp.int32, (down_half, LANES), 1) < LANES // 2
        near_up = lax.broadcasted_iota(jnp.int32, (up_half, LANES), 1) < LANES // 2

        def pack(peer, carry):
            at = pl.multiple_of(peer * feature_rows, 2 * GROUP)
            part = product_down[pl.ds(at, down_half), :]
            other = product_down[pl.ds(at + down_half, down_half), :]
            grad_send[m, peer, 0:down_half, :] = jnp.where(near, part, other)
            at = pl.multiple_of(peer * value_rows, GROUP)
            part = product_up[pl.ds(at, value_rows), :]
            part = jnp.where(near_up, part[0:up_half], part[up_half:value_rows])
            if packed - down_half > up_half:
                rest = jnp.zeros((packed - down_half - up_half, LANES), F32)
                part = jnp.concatenate([part, rest], axis=0)
            grad_send[m, peer, down_half:packed, :] = part.astype(BF16)
            return carry

        lax.fori_loop(0, peers, pack, 0)
        spread(m, grad_send, grad_recv, grad_send_sem, grad_recv_sem)

    def turn():
        def one(index, carry):
            at = pl.ds(pl.multiple_of(index * TILE, TILE), TILE)
            out_turned[at, :] = out_ref[:, at].T
            value_turned[:, at] = value_ref[at, :].T
            return carry

        lax.fori_loop(0, width // TILE, one, 0)

    lag = jnp.where(first, chunks, jnp.where(last, 0, (sections - 1 - section) * 4))
    lag = jnp.minimum(lag, chunks)

    loads[3].wait()
    turn_at = jnp.where(first, chunks, 0)

    drawn = jnp.minimum(jnp.maximum(lag + per_block, chunks + 1), chunks + lag) - 1

    def step(t, carry):
        @pl.when(t == turn_at)
        def _():
            turn()
            lax.fori_loop(0, jnp.where(last, chunks, 0), pull, 0)

        @pl.when((section > 0) & (t < micro))
        def _():
            unpack(t)

        @pl.when(t < chunks)
        def _():
            forward(t)

        c = t - lag

        @pl.when((c >= 0) & (c < chunks))
        def _():
            lax.fori_loop(c, jnp.where(last, c, c + 1), pull, 0)
            backward(c)

        @pl.when(t == drawn)
        def _():
            products(0)

        @pl.when(t == chunks + lag - 1)
        def _():
            products(1)

        return carry

    lax.fori_loop(0, chunks + lag, step, 0)

    for m in range(micro):
        wait_for(grad_recv.at[m], grad_recv_sem.at[m])
        for source, sem in ((panel_send, panel_send_sem), (grad_send, grad_send_sem)):
            wait_for(source.at[m, 0 : peers - 1], sem.at[m])

    @pl.when(section < sections - 1)
    def _():
        for c in range(chunks):
            for piece in range(PIECES):
                part = h_out.at[pl.ds(c * CHUNK, CHUNK), pieces[piece]]
                wait_for(part, h_send_sem.at[c, piece])

    @pl.when(section > 0)
    def _():
        for c in range(chunks):
            for piece in range(PIECES):
                part = g_out.at[pl.ds(c * CHUNK, CHUNK), pieces[piece]]
                wait_for(part, g_send_sem.at[c, piece])


def run_chain(tokens, cotangent, gains, w_value, w_out, down, up, criterion, slot_of):
    micro = criterion.shape[0]
    peers = lax.axis_size("dp")
    rows, width = tokens.shape
    value_width = w_out.shape[0]
    chunks = rows // CHUNK
    slots = down.shape[2]
    useful = (down.shape[0] + up.shape[0]) // 2
    packed = (useful + 15) // 16 * 16
    block = rows // micro
    spaces = [pl.BlockSpec(memory_space=pl.ANY)] * 2
    spaces += [pl.BlockSpec(memory_space=pltpu.VMEM)]
    spaces += [pl.BlockSpec(memory_space=pl.ANY)] * 4
    spaces += [pl.BlockSpec(memory_space=pltpu.SMEM)] * 2
    row_buffer = pltpu.VMEM((rows, width), BF16)
    exchange = (micro, peers, packed, LANES)
    return pl.pallas_call(
        chain_kernel,
        out_shape=jax.ShapeDtypeStruct(exchange, BF16),
        in_specs=spaces,
        out_specs=pl.BlockSpec(memory_space=pl.ANY),
        scratch_shapes=[
            pltpu.VMEM(w_value.shape, BF16),
            pltpu.VMEM(w_out.shape, BF16),
            pltpu.VMEM(w_out.shape, BF16),
            pltpu.VMEM(w_value.shape, BF16),
            pltpu.VMEM(down.shape, BF16),
            pltpu.VMEM(up.shape, BF16),
            pltpu.VMEM((micro * criterion.shape[1], slots), F32),
            row_buffer,
            row_buffer,
            row_buffer,
            row_buffer,
            row_buffer,
            pltpu.VMEM((rows, LANES), F32),
            pltpu.VMEM((rows, value_width), F32),
            pltpu.VMEM((rows, LANES), F32),
            pltpu.VMEM((rows, value_width), BF16),
            pltpu.VMEM((rows, LANES), BF16),
            pltpu.VMEM((rows, LANES), BF16),
            pltpu.VMEM(exchange, BF16),
            pltpu.VMEM(exchange, BF16),
            pltpu.VMEM((micro, width, LANES), BF16),
            pltpu.VMEM((micro, value_width, LANES), BF16),
            pltpu.VMEM((width, LANES), BF16),
            pltpu.VMEM((value_width, LANES), F32),
            pltpu.VMEM(exchange, BF16),
            pltpu.SemaphoreType.DMA((4,)),
            pltpu.SemaphoreType.DMA((chunks, PIECES)),
            pltpu.SemaphoreType.DMA((chunks, PIECES)),
            pltpu.SemaphoreType.DMA((chunks, PIECES)),
            pltpu.SemaphoreType.DMA((chunks, PIECES)),
            pltpu.SemaphoreType.DMA((micro,)),
            pltpu.SemaphoreType.DMA((micro,)),
            pltpu.SemaphoreType.DMA((micro,)),
            pltpu.SemaphoreType.DMA((micro,)),
        ],
        compiler_params=pltpu.CompilerParams(
            collective_id=0, has_side_effects=True, vmem_limit_bytes=56 * 1024 * 1024
        ),
        name="chain",
    )(tokens, cotangent, gains, w_value, w_out, down, up, criterion, slot_of)


def place_kernel(criterion, slot_of, parts, down, up, picks, held, sems):
    step = pl.program_id(0)
    pairs = parts.shape[0]
    up_half = up.shape[0] // 2

    def load(index):
        rows = pl.ds(pl.multiple_of(index * GROUP, GROUP), GROUP)
        return pltpu.make_async_copy(parts.at[:, rows], held.at[index], sems.at[index])

    @pl.when(step == 0)
    def _():
        for index in range(held.shape[0]):
            load(index).start()
        fill_picks(picks, criterion, slot_of)

    load(step).wait()
    chosen = picks[...].astype(BF16)
    flat = held[step].reshape(pairs, GROUP * LANES)
    summed = dot_tn(flat, chosen).reshape(GROUP, 2, LANES // 2, picks.shape[1])

    @pl.when(step < pl.num_programs(0) - 1)
    def _():
        down[0] = summed[:, 0]
        down[1] = summed[:, 1]

    @pl.when(step == pl.num_programs(0) - 1)
    def _():
        up[0:up_half] = summed[0:up_half, 0]
        up[up_half : 2 * up_half] = summed[0:up_half, 1]


def place(criterion, slot_of, parts, feature_rows, value_rows, slots, rank):
    pairs = parts.shape[0]
    down_half = feature_rows // 2
    steps = down_half // GROUP
    down, up = pl.pallas_call(
        place_kernel,
        grid=(steps + 1,),
        in_specs=[
            pl.BlockSpec(memory_space=pltpu.SMEM),
            pl.BlockSpec(memory_space=pltpu.SMEM),
            pl.BlockSpec(memory_space=pltpu.HBM),
        ],
        out_specs=[
            pl.BlockSpec((2, GROUP, rank, slots), lambda i: (0, jnp.minimum(i, steps - 1), 0, 0)),
            pl.BlockSpec((value_rows, rank, slots), lambda i: (0, 0, 0)),
        ],
        out_shape=[
            jax.ShapeDtypeStruct((2, down_half, rank, slots), F32),
            jax.ShapeDtypeStruct((value_rows, rank, slots), F32),
        ],
        scratch_shapes=[
            pltpu.VMEM((pairs, slots), F32),
            pltpu.VMEM((steps + 1, pairs, GROUP, LANES), BF16),
            pltpu.SemaphoreType.DMA((steps + 1,)),
        ],
        compiler_params=pltpu.CompilerParams(vmem_limit_bytes=60 * 1024 * 1024),
        name="place",
    )(criterion, slot_of, parts)
    return down.reshape(feature_rows, rank, slots), up


def on_device(
    tokens,
    cotangent,
    norm_gain,
    value_weight,
    out_weight,
    adapter_down,
    adapter_up,
    criterion,
    slot_of,
):
    micro, block, width = tokens.shape
    down = jnp.transpose(adapter_down[0], (1, 2, 0))
    up = jnp.transpose(adapter_up[0], (1, 2, 0))
    parts = run_chain(
        tokens.reshape(micro * block, width),
        cotangent.reshape(micro * block, width),
        norm_gain,
        value_weight[0],
        out_weight[0],
        down,
        up,
        criterion,
        slot_of,
    )
    parts = parts.reshape((parts.shape[0] * parts.shape[1],) + parts.shape[2:])
    grad_down, grad_up = place(
        criterion, slot_of, parts, down.shape[0], up.shape[0], down.shape[2], down.shape[1]
    )
    return (jnp.transpose(grad_down, (2, 0, 1))[None], jnp.transpose(grad_up, (2, 0, 1))[None])


def solution(mesh):
    return jax.shard_map(
        on_device,
        mesh=mesh,
        in_specs=(
            P(None, "dp", None),
            P(None, "dp", None),
            P("section", None),
            P("section", None, None),
            P("section", None, None),
            P("section", None, "dp", None),
            P("section", None, "dp", None),
            P(),
            P(),
        ),
        out_specs=(P("section", None, "dp", None), P("section", None, "dp", None)),
        check_vma=False,
    )
```

```python
import jax
import jax.numpy as jnp
from jax import lax
from jax.experimental import pallas as pl
from jax.experimental.pallas import tpu as pltpu
from jax.sharding import PartitionSpec as P

EPSILON = 1e-06
CHUNK = 16
TILE = 512
GROUP = 16
PIECES = 2
LANES = 128
BF16 = jnp.bfloat16
F32 = jnp.float32


def dot(left, right):
    return jnp.dot(left, right, preferred_element_type=F32)


def dot_nt(left, right):
    return lax.dot_general(left, right, (((1,), (1,)), ((), ())), preferred_element_type=F32)


def dot_tn(left, right):
    return lax.dot_general(left, right, (((0,), (0,)), ((), ())), preferred_element_type=F32)


def swap_halves(value):
    half = value.shape[-1] // 2
    return jnp.concatenate([value[:, half:], value[:, :half]], axis=1)


def fill_picks(picks, criterion, slot_of):
    micro, blocks = criterion.shape
    lanes = lax.broadcasted_iota(jnp.int32, (1, picks.shape[1]), 1)
    for index in range(micro * blocks):
        slot = slot_of[criterion[index // blocks, index % blocks]]
        picks[index : index + 1, :] = jnp.where(lanes == slot, 1.0, 0.0)


def chain_kernel(
    tokens,
    cotangent,
    gains,
    w_value,
    w_out,
    down,
    up,
    criterion,
    slot_of,
    grad_recv,
    picks,
    value_ref,
    out_ref,
    value_turned,
    out_turned,
    down_ref,
    up_ref,
    h_in,
    h_out,
    g_in,
    g_out,
    scaled,
    inverse,
    mixed_ref,
    narrow_ref,
    value_grad,
    low,
    low_grad,
    panel_send,
    panel_recv,
    panel_down,
    panel_up,
    lifted,
    product_up,
    grad_send,
    load_sem,
    h_send_sem,
    h_recv_sem,
    g_send_sem,
    g_recv_sem,
    panel_send_sem,
    panel_recv_sem,
    grad_send_sem,
    grad_recv_sem,
):
    sections = lax.axis_size("section")
    peers = lax.axis_size("dp")
    section = lax.axis_index("section")
    me = lax.axis_index("dp")
    micro = criterion.shape[0]
    rows, width = h_in.shape
    block = rows // micro
    chunks = rows // CHUNK
    per_block = block // CHUNK
    slots = picks.shape[1]
    feature_rows = down.shape[0]
    value_rows = up.shape[0]
    down_half = feature_rows // 2
    up_half = value_rows // 2
    packed = panel_send.shape[2]
    value_width = value_grad.shape[1]
    piece_width = width // PIECES
    pieces = [slice(start, start + piece_width) for start in range(0, width, piece_width)]
    first = section == 0
    last = section == sections - 1

    loads = [
        pltpu.make_async_copy(source, target, load_sem.at[place])
        for place, (source, target) in enumerate(
            [(down, down_ref), (up, up_ref), (w_value, value_ref), (w_out, out_ref)]
        )
    ]
    loads[0].start()
    loads[1].start()

    def tiles_of(piece):
        base = piece * piece_width
        return [slice(base + at, base + at + TILE) for at in range(0, piece_width, TILE)]

    def chunk_rows(c):
        return pl.ds(pl.multiple_of(c * CHUNK, CHUNK), CHUNK)

    barrier = pltpu.get_barrier_semaphore()

    def greet(k, carry):
        pl.semaphore_signal(
            barrier,
            inc=1,
            device_id={"dp": lax.rem(me + k, peers)},
            device_id_type=pl.DeviceIdType.MESH,
        )
        return carry

    lax.fori_loop(1, peers, greet, 0)
    for step in (1, sections - 1):
        pl.semaphore_signal(
            barrier,
            inc=1,
            device_id={"section": lax.rem(section + step, sections)},
            device_id_type=pl.DeviceIdType.MESH,
        )

    fill_picks(picks, criterion, slot_of)
    chosen = picks[...].astype(BF16)
    loads[0].wait()
    loads[1].wait()
    loads[2].start()

    @pl.when(first)
    def _():
        for c in range(chunks):
            part = pl.ds(c * CHUNK, CHUNK)
            for piece in range(PIECES):
                pltpu.make_async_copy(
                    tokens.at[part, pieces[piece]],
                    h_in.at[part, pieces[piece]],
                    h_recv_sem.at[c, piece],
                ).start()

    @pl.when(last)
    def _():
        for c in range(chunks):
            part = pl.ds(c * CHUNK, CHUNK)
            for piece in range(PIECES):
                pltpu.make_async_copy(
                    cotangent.at[part, pieces[piece]],
                    g_in.at[part, pieces[piece]],
                    g_recv_sem.at[c, piece],
                ).start()

    loads[3].start()
    for start in range(0, down_half, GROUP):
        pair = jnp.concatenate(
            [down_ref[start : start + GROUP], down_ref[down_half + start : down_half + start + GROUP]],
            axis=1,
        )
        found = dot_nt(chosen, pair.reshape(GROUP * LANES, slots))
        found = found.reshape(micro, peers, GROUP, LANES).astype(BF16)
        panel_send[:, :, start : start + GROUP, :] = found
    pair = jnp.concatenate([up_ref[0:up_half], up_ref[up_half:value_rows]], axis=1)
    found = dot_nt(chosen, pair.reshape(up_half * LANES, slots)).reshape(
        micro, peers, up_half, LANES
    )
    if packed - down_half > up_half:
        rest = jnp.zeros((micro, peers, packed - down_half - up_half, LANES), F32)
        found = jnp.concatenate([found, rest], axis=2)
    panel_send[:, :, down_half:packed, :] = found.astype(BF16)

    pl.semaphore_wait(barrier, peers + 1)

    def hand(m, peer, source, target, send_sem, recv_sem):
        pltpu.make_async_remote_copy(
            src_ref=source.at[m, peer],
            dst_ref=target.at[m, me],
            send_sem=send_sem.at[m],
            recv_sem=recv_sem.at[m],
            device_id={"dp": peer},
            device_id_type=pl.DeviceIdType.MESH,
        ).start()

    def keep(m, source, target, recv_sem):
        pltpu.make_async_copy(source.at[m, me], target.at[m, me], recv_sem.at[m]).start()

    def spread(m, source, target, send_sem, recv_sem):
        def send(k, carry):
            hand(m, lax.rem(me + k, peers), source, target, send_sem, recv_sem)
            return carry

        keep(m, source, target, recv_sem)
        lax.fori_loop(1, peers, send, 0)

    def wait_for(ref, sem):
        pltpu.make_async_copy(ref, ref, sem).wait()

    spread(0, panel_send, panel_recv, panel_send_sem, panel_recv_sem)

    loads[2].wait()

    near = lax.broadcasted_iota(jnp.int32, (down_half, LANES), 1) < LANES // 2
    near_up = near[0:up_half]
    near_row = near[0:CHUNK]

    def unpack(m):
        wait_for(panel_recv.at[m], panel_recv_sem.at[m])

        @pl.when(m < micro - 1)
        def _():
            spread(m + 1, panel_send, panel_recv, panel_send_sem, panel_recv_sem)

        def one(source, carry):
            at = pl.multiple_of(source * feature_rows, 2 * GROUP)
            part = panel_recv[m, source, 0:down_half, :]
            other = panel_recv[m, source + peers // 2, 0:down_half, :]
            crossed = swap_halves(jnp.where(near, other, part))
            panel_down[m, pl.ds(at, down_half), :] = jnp.where(near, part, crossed)
            panel_down[m, pl.ds(at + down_half, down_half), :] = jnp.where(near, crossed, other)
            for place in (source, source + peers // 2):
                at = pl.multiple_of(place * value_rows, GROUP)
                part = panel_recv[m, place, down_half:packed, :].astype(F32)[0:up_half]
                both = [jnp.where(near_up, part, 0.0), jnp.where(near_up, 0.0, part)]
                panel_up[m, pl.ds(at, value_rows), :] = jnp.concatenate(both, axis=0).astype(BF16)
            return carry

        lax.fori_loop(0, peers // 2, one, 0)

    def send_piece(source, target, c, piece, send_sem, recv_sem, to):
        here = chunk_rows(c)
        columns = pieces[piece]
        pltpu.make_async_remote_copy(
            src_ref=source.at[here, columns],
            dst_ref=target.at[here, columns],
            send_sem=send_sem.at[c, piece],
            recv_sem=recv_sem.at[c, piece],
            device_id={"section": to},
            device_id_type=pl.DeviceIdType.MESH,
        ).start()

    def forward(c):
        m = c // per_block
        here = chunk_rows(c)
        squares = jnp.zeros((CHUNK, LANES), F32)
        mixed = jnp.zeros((CHUNK, value_width), F32)
        for piece in range(PIECES):
            wait_for(h_in.at[here, pieces[piece]], h_recv_sem.at[c, piece])
            for tile in tiles_of(piece):
                hidden = h_in[here, tile].astype(F32)
                square = hidden * hidden
                for start in range(0, TILE, LANES):
                    squares += square[:, start : start + LANES]
                part = (hidden * gains[:, tile]).astype(BF16)
                scaled[here, tile] = part
                mixed += dot(part, value_ref[tile, :])
        total = jnp.sum(squares, axis=1, keepdims=True)
        factor = lax.rsqrt(total / width + EPSILON)
        inverse[here, :] = jnp.broadcast_to(factor, (CHUNK, LANES))
        mixed_ref[here, :] = mixed

        @pl.when(first & (c % per_block == 0))
        def _():
            unpack(m)

        narrow = jnp.zeros((2 * CHUNK, LANES), F32)
        for tile, far in zip(tiles_of(0), tiles_of(1)):
            both = jnp.concatenate([scaled[here, tile], scaled[here, far]], axis=0)
            narrow += dot(both, panel_down[m, tile, :])
        narrow = jnp.where(near_row, narrow[0:CHUNK], narrow[CHUNK : 2 * CHUNK])
        narrow_ref[here, :] = narrow
        narrow = ((narrow + swap_halves(narrow)) * factor).astype(BF16)
        low[here, :] = narrow

        @pl.when(section < sections - 1)
        def _():
            values = (mixed * factor + dot_nt(narrow, panel_up[m])).astype(BF16)
            for piece in range(PIECES):
                for tile in tiles_of(piece):
                    added = dot(values, out_ref[:, tile])
                    h_out[here, tile] = (h_in[here, tile].astype(F32) + added).astype(BF16)
                send_piece(h_out, h_in, c, piece, h_send_sem, h_recv_sem, section + 1)

    def pull(c, carry):
        here = chunk_rows(c)
        pulled = jnp.zeros((CHUNK, value_width), F32)
        for piece in range(PIECES):
            wait_for(g_in.at[here, pieces[piece]], g_recv_sem.at[c, piece])
            for tile in tiles_of(piece):
                pulled += dot(g_in[here, tile], out_turned[tile, :])
        value_grad[here, :] = pulled.astype(BF16)
        return carry

    def backward(c):
        m = c // per_block
        here = chunk_rows(c)
        pulled = value_grad[here, :]
        narrow = dot(pulled, panel_up[m])
        narrow = narrow + swap_halves(narrow)
        factor = inverse[here, 0:1]
        low_grad[here, :] = (narrow * factor).astype(BF16)

        @pl.when(section > 0)
        def _():
            held = narrow.astype(BF16)
            along = pulled.astype(F32) * mixed_ref[here, :]
            moment = jnp.sum(along, axis=1, keepdims=True)
            along = held.astype(F32) * narrow_ref[here, :]
            moment += jnp.sum(along, axis=1, keepdims=True)
            bend = factor * factor * factor * (moment / width)
            none = jnp.zeros_like(held)
            both = [jnp.where(near_row, held, none), jnp.where(near_row, none, held)]
            both = jnp.concatenate(both, axis=0)
            for tile in tiles_of(0):
                lifted[:, tile] = dot_nt(both, panel_down[m, tile, :])
            for piece in range(PIECES):
                for near_tile, tile in zip(tiles_of(0), tiles_of(piece)):
                    part = dot(pulled, value_turned[:, tile])
                    part += lifted[piece * CHUNK : (piece + 1) * CHUNK, near_tile]
                    result = (
                        g_in[here, tile].astype(F32)
                        + factor * (part * gains[:, tile])
                        - h_in[here, tile].astype(F32) * bend
                    )
                    g_out[here, tile] = result.astype(BF16)
                send_piece(g_out, g_in, c, piece, g_send_sem, g_recv_sem, section - 1)

    def products(m):
        here = pl.ds(pl.multiple_of(m * block, block), block)
        product_up[...] = dot_tn(value_grad[here, :], low[here, :])
        several = min(4, peers)
        span = several * feature_rows

        def group(k, carry):
            which = lax.rem(me // several + k, peers // several)
            columns = pl.ds(pl.multiple_of(which * span, LANES), span)
            product = dot_tn(scaled[here, columns], low_grad[here, :]).astype(BF16)
            for q in range(several):
                peer = which * several + q
                at = q * feature_rows
                part = product[at : at + down_half]
                other = product[at + down_half : at + feature_rows]
                grad_send[m, peer, 0:down_half, :] = jnp.where(near, part, other)
                at = pl.multiple_of(peer * value_rows, GROUP)
                part = product_up[pl.ds(at, value_rows), :]
                part = jnp.where(near_up, part[0:up_half], part[up_half:value_rows])
                if packed - down_half > up_half:
                    rest = jnp.zeros((packed - down_half - up_half, LANES), F32)
                    part = jnp.concatenate([part, rest], axis=0)
                grad_send[m, peer, down_half:packed, :] = part.astype(BF16)

                @pl.when(peer != me)
                def _():
                    hand(m, peer, grad_send, grad_recv, grad_send_sem, grad_recv_sem)

                @pl.when(peer == me)
                def _():
                    keep(m, grad_send, grad_recv, grad_recv_sem)

            return carry

        lax.fori_loop(0, peers // several, group, 0)

    def turn():
        def one(index, carry):
            at = pl.ds(pl.multiple_of(index * TILE, TILE), TILE)
            out_turned[at, :] = out_ref[:, at].T
            value_turned[:, at] = value_ref[at, :].T
            return carry

        lax.fori_loop(0, width // TILE, one, 0)

    lag = jnp.where(first, chunks, jnp.where(last, 0, (sections - 1 - section) * 4))
    lag = jnp.minimum(lag, chunks)

    loads[3].wait()
    turn_at = jnp.where(first, chunks, 0)

    drawn = jnp.minimum(jnp.maximum(lag + per_block, chunks + 1), chunks + lag) - 1

    def step(t, carry):
        @pl.when(t == turn_at)
        def _():
            turn()
            lax.fori_loop(0, jnp.where(last, chunks, 0), pull, 0)

        @pl.when((section > 0) & ((t == 0) | (t == per_block // 2)))
        def _():
            unpack(jnp.where(t == 0, 0, 1))

        @pl.when(t < chunks)
        def _():
            forward(t)

        c = t - lag

        @pl.when((c >= 0) & (c < chunks))
        def _():
            lax.fori_loop(c, jnp.where(last, c, c + 1), pull, 0)
            backward(c)

        @pl.when(t == drawn)
        def _():
            products(0)

        @pl.when(t == chunks + lag - 1)
        def _():
            products(1)

        return carry

    lax.fori_loop(0, chunks + lag, step, 0)

    for m in range(micro):
        wait_for(grad_recv.at[m], grad_recv_sem.at[m])
        for source, sem in ((panel_send, panel_send_sem), (grad_send, grad_send_sem)):
            wait_for(source.at[m, 0 : peers - 1], sem.at[m])

    @pl.when(section < sections - 1)
    def _():
        for c in range(chunks):
            for piece in range(PIECES):
                part = h_out.at[pl.ds(c * CHUNK, CHUNK), pieces[piece]]
                wait_for(part, h_send_sem.at[c, piece])

    @pl.when(section > 0)
    def _():
        for c in range(chunks):
            for piece in range(PIECES):
                part = g_out.at[pl.ds(c * CHUNK, CHUNK), pieces[piece]]
                wait_for(part, g_send_sem.at[c, piece])


def run_chain(tokens, cotangent, gains, w_value, w_out, down, up, criterion, slot_of):
    micro = criterion.shape[0]
    peers = lax.axis_size("dp")
    rows, width = tokens.shape
    value_width = w_out.shape[0]
    chunks = rows // CHUNK
    slots = down.shape[2]
    useful = (down.shape[0] + up.shape[0]) // 2
    packed = (useful + 15) // 16 * 16
    block = rows // micro
    spaces = [pl.BlockSpec(memory_space=pl.ANY)] * 2
    spaces += [pl.BlockSpec(memory_space=pltpu.VMEM)]
    spaces += [pl.BlockSpec(memory_space=pl.ANY)] * 4
    spaces += [pl.BlockSpec(memory_space=pltpu.SMEM)] * 2
    row_buffer = pltpu.VMEM((rows, width), BF16)
    exchange = (micro, peers, packed, LANES)
    return pl.pallas_call(
        chain_kernel,
        out_shape=[
            jax.ShapeDtypeStruct(exchange, BF16),
            jax.ShapeDtypeStruct((micro * criterion.shape[1], slots), F32),
        ],
        in_specs=spaces,
        out_specs=[
            pl.BlockSpec(memory_space=pl.ANY),
            pl.BlockSpec(memory_space=pltpu.VMEM),
        ],
        scratch_shapes=[
            pltpu.VMEM(w_value.shape, BF16),
            pltpu.VMEM(w_out.shape, BF16),
            pltpu.VMEM(w_out.shape, BF16),
            pltpu.VMEM(w_value.shape, BF16),
            pltpu.VMEM(down.shape, BF16),
            pltpu.VMEM(up.shape, BF16),
            row_buffer,
            row_buffer,
            row_buffer,
            row_buffer,
            row_buffer,
            pltpu.VMEM((rows, LANES), F32),
            pltpu.VMEM((rows, value_width), F32),
            pltpu.VMEM((rows, LANES), F32),
            pltpu.VMEM((rows, value_width), BF16),
            pltpu.VMEM((rows, LANES), BF16),
            pltpu.VMEM((rows, LANES), BF16),
            pltpu.VMEM(exchange, BF16),
            pltpu.VMEM(exchange, BF16),
            pltpu.VMEM((micro, width // 2, LANES), BF16),
            pltpu.VMEM((micro, value_width, LANES), BF16),
            pltpu.VMEM((2 * CHUNK, width // 2), F32),
            pltpu.VMEM((value_width, LANES), F32),
            pltpu.VMEM(exchange, BF16),
            pltpu.SemaphoreType.DMA((4,)),
            pltpu.SemaphoreType.DMA((chunks, PIECES)),
            pltpu.SemaphoreType.DMA((chunks, PIECES)),
            pltpu.SemaphoreType.DMA((chunks, PIECES)),
            pltpu.SemaphoreType.DMA((chunks, PIECES)),
            pltpu.SemaphoreType.DMA((micro,)),
            pltpu.SemaphoreType.DMA((micro,)),
            pltpu.SemaphoreType.DMA((micro,)),
            pltpu.SemaphoreType.DMA((micro,)),
        ],
        compiler_params=pltpu.CompilerParams(
            collective_id=0, has_side_effects=True, vmem_limit_bytes=56 * 1024 * 1024
        ),
        name="chain",
    )(tokens, cotangent, gains, w_value, w_out, down, up, criterion, slot_of)


def place_kernel(picks, parts, down, up, chosen, held, down_out, up_out, pick_sem, load_sem, store_sem):
    pairs = parts.shape[0]
    groups = held.shape[0]
    up_half = up.shape[0] // 2
    half = down.shape[0] // 2
    pick_load = pltpu.make_async_copy(picks, chosen, pick_sem)
    pick_load.start()
    loads = [
        pltpu.make_async_copy(
            parts.at[:, pl.ds(index * GROUP, GROUP)], held.at[index], load_sem.at[index]
        )
        for index in range(groups)
    ]
    for load in loads:
        load.start()
    pick_load.wait()
    stores = []
    for index in range(groups):
        loads[index].wait()
        flat = held[index].reshape(pairs, GROUP * LANES)
        summed = dot_tn(flat, chosen[...].astype(BF16))
        summed = summed.reshape(GROUP, 2, LANES // 2, chosen.shape[1])
        for side in range(2):
            if index < groups - 1:
                at = pl.ds(side * half + index * GROUP, GROUP)
                down_out[at] = summed[:, side]
                store = pltpu.make_async_copy(
                    down_out.at[at], down.at[at], store_sem.at[index, side]
                )
            else:
                at = pl.ds(side * up_half, up_half)
                up_out[at] = summed[0:up_half, side]
                store = pltpu.make_async_copy(up_out.at[at], up.at[at], store_sem.at[index, side])
            store.start()
            stores.append(store)
    for store in stores:
        store.wait()


def place(picks, parts, feature_rows, value_rows, rank):
    pairs, packed = parts.shape[0:2]
    slots = picks.shape[1]
    groups = packed // GROUP
    down_shape = (feature_rows, rank, slots)
    up_shape = (value_rows, rank, slots)
    return pl.pallas_call(
        place_kernel,
        in_specs=[pl.BlockSpec(memory_space=pltpu.HBM)] * 2,
        out_specs=[pl.BlockSpec(memory_space=pl.ANY)] * 2,
        out_shape=[
            jax.ShapeDtypeStruct(down_shape, F32),
            jax.ShapeDtypeStruct(up_shape, F32),
        ],
        scratch_shapes=[
            pltpu.VMEM((pairs, slots), F32),
            pltpu.VMEM((groups, pairs, GROUP, LANES), BF16),
            pltpu.VMEM(down_shape, F32),
            pltpu.VMEM(up_shape, F32),
            pltpu.SemaphoreType.DMA,
            pltpu.SemaphoreType.DMA((groups,)),
            pltpu.SemaphoreType.DMA((groups, 2)),
        ],
        compiler_params=pltpu.CompilerParams(vmem_limit_bytes=60 * 1024 * 1024),
        name="place",
    )(picks, parts)


def on_device(
    tokens,
    cotangent,
    norm_gain,
    value_weight,
    out_weight,
    adapter_down,
    adapter_up,
    criterion,
    slot_of,
):
    micro, block, width = tokens.shape
    down = jnp.transpose(adapter_down[0], (1, 2, 0))
    up = jnp.transpose(adapter_up[0], (1, 2, 0))
    parts, picks = run_chain(
        tokens.reshape(micro * block, width),
        cotangent.reshape(micro * block, width),
        norm_gain,
        value_weight[0],
        out_weight[0],
        down,
        up,
        criterion,
        slot_of,
    )
    parts = parts.reshape((parts.shape[0] * parts.shape[1],) + parts.shape[2:])
    grad_down, grad_up = place(picks, parts, down.shape[0], up.shape[0], down.shape[1])
    return (jnp.transpose(grad_down, (2, 0, 1))[None], jnp.transpose(grad_up, (2, 0, 1))[None])


def solution(mesh):
    return jax.shard_map(
        on_device,
        mesh=mesh,
        in_specs=(
            P(None, "dp", None),
            P(None, "dp", None),
            P("section", None),
            P("section", None, None),
            P("section", None, None),
            P("section", None, "dp", None),
            P("section", None, "dp", None),
            P(),
            P(),
        ),
        out_specs=(P("section", None, "dp", None), P("section", None, "dp", None)),
        check_vma=False,
    )
```

```python
import jax
import jax.numpy as jnp
from jax import lax
from jax.experimental import pallas as pl
from jax.experimental.pallas import tpu as pltpu
from jax.sharding import PartitionSpec as P

EPSILON = 1e-06
CHUNK = 16
TILE = 512
GROUP = 16
PIECES = 2
LANES = 128
BF16 = jnp.bfloat16
F32 = jnp.float32


def dot(left, right):
    return jnp.dot(left, right, preferred_element_type=F32)


def dot_nt(left, right):
    return lax.dot_general(left, right, (((1,), (1,)), ((), ())), preferred_element_type=F32)


def dot_tn(left, right):
    return lax.dot_general(left, right, (((0,), (0,)), ((), ())), preferred_element_type=F32)


def swap_halves(value):
    half = value.shape[-1] // 2
    return jnp.concatenate([value[:, half:], value[:, :half]], axis=1)


def fill_picks(picks, criterion, slot_of):
    micro, blocks = criterion.shape
    lanes = lax.broadcasted_iota(jnp.int32, (1, picks.shape[1]), 1)
    for index in range(micro * blocks):
        slot = slot_of[criterion[index // blocks, index % blocks]]
        picks[index : index + 1, :] = jnp.where(lanes == slot, 1.0, 0.0)


def chain_kernel(
    tokens,
    cotangent,
    gains,
    w_value,
    w_out,
    down,
    up,
    criterion,
    slot_of,
    grad_recv,
    picks,
    value_ref,
    out_ref,
    value_turned,
    out_turned,
    down_ref,
    up_ref,
    h_in,
    h_out,
    g_in,
    g_out,
    scaled,
    inverse,
    mixed_ref,
    narrow_ref,
    value_grad,
    low,
    low_grad,
    panel_send,
    panel_recv,
    panel_down,
    panel_up,
    product_up,
    grad_send,
    load_sem,
    h_send_sem,
    h_recv_sem,
    g_send_sem,
    g_recv_sem,
    panel_send_sem,
    panel_recv_sem,
    grad_send_sem,
    grad_recv_sem,
):
    sections = lax.axis_size("section")
    peers = lax.axis_size("dp")
    section = lax.axis_index("section")
    me = lax.axis_index("dp")
    micro = criterion.shape[0]
    rows, width = h_in.shape
    block = rows // micro
    chunks = rows // CHUNK
    per_block = block // CHUNK
    slots = picks.shape[1]
    feature_rows = down.shape[0]
    value_rows = up.shape[0]
    down_half = feature_rows // 2
    up_half = value_rows // 2
    packed = panel_send.shape[2]
    value_width = value_grad.shape[1]
    piece_width = width // PIECES
    pieces = [slice(start, start + piece_width) for start in range(0, width, piece_width)]
    first = section == 0
    last = section == sections - 1

    loads = [
        pltpu.make_async_copy(source, target, load_sem.at[place])
        for place, (source, target) in enumerate(
            [(down, down_ref), (up, up_ref), (w_value, value_ref), (w_out, out_ref)]
        )
    ]
    loads[0].start()
    loads[1].start()

    def tiles_of(piece):
        base = piece * piece_width
        return [slice(base + at, base + at + TILE) for at in range(0, piece_width, TILE)]

    def chunk_rows(c):
        return pl.ds(pl.multiple_of(c * CHUNK, CHUNK), CHUNK)

    barrier = pltpu.get_barrier_semaphore()

    def greet(k, carry):
        pl.semaphore_signal(
            barrier,
            inc=1,
            device_id={"dp": lax.rem(me + k, peers)},
            device_id_type=pl.DeviceIdType.MESH,
        )
        return carry

    lax.fori_loop(1, peers, greet, 0)
    for step in (1, sections - 1):
        pl.semaphore_signal(
            barrier,
            inc=1,
            device_id={"section": lax.rem(section + step, sections)},
            device_id_type=pl.DeviceIdType.MESH,
        )

    fill_picks(picks, criterion, slot_of)
    chosen = picks[...].astype(BF16)
    loads[0].wait()
    loads[1].wait()
    loads[2].start()

    @pl.when(first)
    def _():
        for c in range(chunks):
            part = pl.ds(c * CHUNK, CHUNK)
            for piece in range(PIECES):
                pltpu.make_async_copy(
                    tokens.at[part, pieces[piece]],
                    h_in.at[part, pieces[piece]],
                    h_recv_sem.at[c, piece],
                ).start()

    @pl.when(last)
    def _():
        for c in range(chunks):
            part = pl.ds(c * CHUNK, CHUNK)
            for piece in range(PIECES):
                pltpu.make_async_copy(
                    cotangent.at[part, pieces[piece]],
                    g_in.at[part, pieces[piece]],
                    g_recv_sem.at[c, piece],
                ).start()

    loads[3].start()
    for start in range(0, down_half, GROUP):
        pair = jnp.concatenate(
            [down_ref[start : start + GROUP], down_ref[down_half + start : down_half + start + GROUP]],
            axis=1,
        )
        found = dot_nt(chosen, pair.reshape(GROUP * LANES, slots))
        found = found.reshape(micro, peers, GROUP, LANES).astype(BF16)
        panel_send[:, :, start : start + GROUP, :] = found
    pair = jnp.concatenate([up_ref[0:up_half], up_ref[up_half:value_rows]], axis=1)
    found = dot_nt(chosen, pair.reshape(up_half * LANES, slots)).reshape(
        micro, peers, up_half, LANES
    )
    if packed - down_half > up_half:
        rest = jnp.zeros((micro, peers, packed - down_half - up_half, LANES), F32)
        found = jnp.concatenate([found, rest], axis=2)
    panel_send[:, :, down_half:packed, :] = found.astype(BF16)

    pl.semaphore_wait(barrier, peers + 1)

    def hand(m, peer, source, target, send_sem, landed):
        pltpu.make_async_remote_copy(
            src_ref=source.at[m, peer],
            dst_ref=target.at[m, me],
            send_sem=send_sem.at[m],
            recv_sem=landed,
            device_id={"dp": peer},
            device_id_type=pl.DeviceIdType.MESH,
        ).start()

    def keep(m, source, target, landed):
        pltpu.make_async_copy(source.at[m, me], target.at[m, me], landed).start()

    def spread_panels(m):
        landed = panel_recv_sem.at[m, me]

        def send(k, carry):
            peer = lax.rem(me + k // 2 + k % 2 * (peers // 2), peers)
            hand(m, peer, panel_send, panel_recv, panel_send_sem, landed)
            return carry

        keep(m, panel_send, panel_recv, landed)
        lax.fori_loop(1, peers, send, 0)

    def wait_for(ref, sem):
        pltpu.make_async_copy(ref, ref, sem).wait()

    spread_panels(0)

    loads[2].wait()

    near = lax.broadcasted_iota(jnp.int32, (down_half, LANES), 1) < LANES // 2
    near_up = near[0:up_half]
    near_row = near[0:CHUNK]

    def unpack(m):
        def one(k, carry):
            source = lax.rem(me - k + peers, peers // 2)
            for place in (source, source + peers // 2):
                wait_for(panel_recv.at[m, place], panel_recv_sem.at[m, place])
            at = pl.multiple_of(source * feature_rows, 2 * GROUP)
            part = panel_recv[m, source, 0:down_half, :]
            other = panel_recv[m, source + peers // 2, 0:down_half, :]
            crossed = swap_halves(jnp.where(near, other, part))
            panel_down[m, pl.ds(at, down_half), :] = jnp.where(near, part, crossed)
            panel_down[m, pl.ds(at + down_half, down_half), :] = jnp.where(near, crossed, other)
            for place in (source, source + peers // 2):
                at = pl.multiple_of(place * value_rows, GROUP)
                part = panel_recv[m, place, down_half:packed, :].astype(F32)[0:up_half]
                both = [jnp.where(near_up, part, 0.0), jnp.where(near_up, 0.0, part)]
                panel_up[m, pl.ds(at, value_rows), :] = jnp.concatenate(both, axis=0).astype(BF16)
            return carry

        lax.fori_loop(0, peers // 2, one, 0)

        @pl.when(m < micro - 1)
        def _():
            spread_panels(m + 1)

    def send_piece(source, target, c, piece, send_sem, recv_sem, to):
        here = chunk_rows(c)
        columns = pieces[piece]
        pltpu.make_async_remote_copy(
            src_ref=source.at[here, columns],
            dst_ref=target.at[here, columns],
            send_sem=send_sem.at[c, piece],
            recv_sem=recv_sem.at[c, piece],
            device_id={"section": to},
            device_id_type=pl.DeviceIdType.MESH,
        ).start()

    def forward(c):
        m = c // per_block
        here = chunk_rows(c)

        @pl.when(first & (c % per_block == 0))
        def _():
            unpack(m)

        squares = jnp.zeros((CHUNK, LANES), F32)
        mixed = jnp.zeros((CHUNK, value_width), F32)
        narrow = jnp.zeros((2 * CHUNK, LANES), F32)
        for piece in range(PIECES):
            wait_for(h_in.at[here, pieces[piece]], h_recv_sem.at[c, piece])
            for tile in tiles_of(piece):
                hidden = h_in[here, tile].astype(F32)
                square = hidden * hidden
                for start in range(0, TILE, LANES):
                    squares += square[:, start : start + LANES]
                scaled[here, tile] = (hidden * gains[:, tile]).astype(BF16)
            if piece == PIECES - 1:
                for tile, far in zip(tiles_of(0), tiles_of(1)):
                    both = jnp.concatenate([scaled[here, tile], scaled[here, far]], axis=0)
                    narrow += dot(both, panel_down[m, tile, :])
            for tile in tiles_of(piece):
                mixed += dot(scaled[here, tile], value_ref[tile, :])
        total = jnp.sum(squares, axis=1, keepdims=True)
        factor = lax.rsqrt(total / width + EPSILON)
        inverse[here, :] = jnp.broadcast_to(factor, (CHUNK, LANES))
        mixed_ref[here, :] = mixed
        narrow = jnp.where(near_row, narrow[0:CHUNK], narrow[CHUNK : 2 * CHUNK])
        narrow_ref[here, :] = narrow
        narrow = ((narrow + swap_halves(narrow)) * factor).astype(BF16)
        low[here, :] = narrow
        values = (mixed * factor + dot_nt(narrow, panel_up[m])).astype(BF16)

        @pl.when(section < sections - 1)
        def _():
            for piece in range(PIECES):
                for tile in tiles_of(piece):
                    added = dot(values, out_ref[:, tile])
                    h_out[here, tile] = (h_in[here, tile].astype(F32) + added).astype(BF16)
                send_piece(h_out, h_in, c, piece, h_send_sem, h_recv_sem, section + 1)

    def pull(c, carry):
        here = chunk_rows(c)
        pulled = jnp.zeros((CHUNK, value_width), F32)
        for piece in range(PIECES):
            wait_for(g_in.at[here, pieces[piece]], g_recv_sem.at[c, piece])
            for tile in tiles_of(piece):
                pulled += dot(g_in[here, tile], out_turned[tile, :])
        value_grad[here, :] = pulled.astype(BF16)
        return carry

    def lower(c, pulled):
        here = chunk_rows(c)
        narrow = dot(pulled, panel_up[c // per_block])
        narrow = narrow + swap_halves(narrow)
        factor = inverse[here, 0:1]
        low_grad[here, :] = (narrow * factor).astype(BF16)
        return narrow.astype(BF16), factor

    def backward(c):
        m = c // per_block
        here = chunk_rows(c)

        @pl.when(first)
        def _():
            lower(c, value_grad[here, :])

        @pl.when(section > 0)
        def _():
            pulled = value_grad[here, :]
            held, factor = lower(c, pulled)
            parts = [dot(pulled, value_turned[:, tile]) for tile in tiles_of(0)]
            along = pulled.astype(F32) * mixed_ref[here, :]
            moment = jnp.sum(along, axis=1, keepdims=True)
            along = held.astype(F32) * narrow_ref[here, :]
            moment += jnp.sum(along, axis=1, keepdims=True)
            bend = factor * factor * factor * (moment / width)
            none = jnp.zeros_like(held)
            both = [jnp.where(near_row, held, none), jnp.where(near_row, none, held)]
            both = jnp.concatenate(both, axis=0)
            lifts = [dot_nt(both, panel_down[m, tile, :]) for tile in tiles_of(0)]
            for piece in range(PIECES):
                if piece > 0:
                    parts = [dot(pulled, value_turned[:, tile]) for tile in tiles_of(piece)]
                for part, lift, tile in zip(parts, lifts, tiles_of(piece)):
                    part += lift[piece * CHUNK : (piece + 1) * CHUNK]
                    result = (
                        g_in[here, tile].astype(F32)
                        + factor * (part * gains[:, tile])
                        - h_in[here, tile].astype(F32) * bend
                    )
                    g_out[here, tile] = result.astype(BF16)
                send_piece(g_out, g_in, c, piece, g_send_sem, g_recv_sem, section - 1)

    def products(m):
        here = pl.ds(pl.multiple_of(m * block, block), block)
        product_up[...] = dot_tn(value_grad[here, :], low[here, :])
        several = min(4, peers)
        span = several * feature_rows

        def group(k, carry):
            which = lax.rem(me // several + k, peers // several)
            columns = pl.ds(pl.multiple_of(which * span, LANES), span)
            product = dot_tn(scaled[here, columns], low_grad[here, :]).astype(BF16)
            for q in range(several):
                peer = which * several + q
                at = q * feature_rows
                part = product[at : at + down_half]
                other = product[at + down_half : at + feature_rows]
                grad_send[m, peer, 0:down_half, :] = jnp.where(near, part, other)
                at = pl.multiple_of(peer * value_rows, GROUP)
                part = product_up[pl.ds(at, value_rows), :]
                part = jnp.where(near_up, part[0:up_half], part[up_half:value_rows])
                if packed - down_half > up_half:
                    rest = jnp.zeros((packed - down_half - up_half, LANES), F32)
                    part = jnp.concatenate([part, rest], axis=0)
                grad_send[m, peer, down_half:packed, :] = part.astype(BF16)

                @pl.when(peer != me)
                def _():
                    hand(m, peer, grad_send, grad_recv, grad_send_sem, grad_recv_sem.at[m])

                @pl.when(peer == me)
                def _():
                    keep(m, grad_send, grad_recv, grad_recv_sem.at[m])

            return carry

        lax.fori_loop(0, peers // several, group, 0)

    def turn():
        def one(index, carry):
            at = pl.ds(pl.multiple_of(index * TILE, TILE), TILE)
            out_turned[at, :] = out_ref[:, at].T
            value_turned[:, at] = value_ref[at, :].T
            return carry

        lax.fori_loop(0, width // TILE, one, 0)

    lag = jnp.where(first, chunks, jnp.where(last, 0, (sections - 1 - section) * 3 + (2 - section)))
    lag = jnp.minimum(lag, chunks)

    loads[3].wait()
    turn_at = jnp.where(first, chunks, 0)

    drawn = jnp.minimum(jnp.maximum(lag + per_block, chunks + 1), chunks + lag) - 1

    def step(t, carry):
        @pl.when(t == turn_at)
        def _():
            turn()
            lax.fori_loop(0, jnp.where(last, chunks, 0), pull, 0)

        @pl.when((section > 0) & ((t == 0) | (t == per_block // 2)))
        def _():
            unpack(jnp.where(t == 0, 0, 1))

        @pl.when(t < chunks)
        def _():
            forward(t)

        c = t - lag

        @pl.when((c >= 0) & (c < chunks))
        def _():
            @pl.when(section < sections - 1)
            def _():
                pull(c, 0)

            backward(c)

        @pl.when(t == drawn)
        def _():
            products(0)

        @pl.when(t == chunks + lag - 1)
        def _():
            products(1)

        return carry

    lax.fori_loop(0, chunks + lag, step, 0)

    for m in range(micro):
        wait_for(grad_recv.at[m], grad_recv_sem.at[m])
        for source, sem in ((panel_send, panel_send_sem), (grad_send, grad_send_sem)):
            wait_for(source.at[m, 0 : peers - 1], sem.at[m])

    @pl.when(section < sections - 1)
    def _():
        for c in range(chunks):
            for piece in range(PIECES):
                part = h_out.at[pl.ds(c * CHUNK, CHUNK), pieces[piece]]
                wait_for(part, h_send_sem.at[c, piece])

    @pl.when(section > 0)
    def _():
        for c in range(chunks):
            for piece in range(PIECES):
                part = g_out.at[pl.ds(c * CHUNK, CHUNK), pieces[piece]]
                wait_for(part, g_send_sem.at[c, piece])


def run_chain(tokens, cotangent, gains, w_value, w_out, down, up, criterion, slot_of):
    micro = criterion.shape[0]
    peers = lax.axis_size("dp")
    rows, width = tokens.shape
    value_width = w_out.shape[0]
    chunks = rows // CHUNK
    slots = down.shape[2]
    useful = (down.shape[0] + up.shape[0]) // 2
    packed = (useful + 15) // 16 * 16
    block = rows // micro
    spaces = [pl.BlockSpec(memory_space=pl.ANY)] * 2
    spaces += [pl.BlockSpec(memory_space=pltpu.VMEM)]
    spaces += [pl.BlockSpec(memory_space=pl.ANY)] * 4
    spaces += [pl.BlockSpec(memory_space=pltpu.SMEM)] * 2
    row_buffer = pltpu.VMEM((rows, width), BF16)
    exchange = (micro, peers, packed, LANES)
    return pl.pallas_call(
        chain_kernel,
        out_shape=[
            jax.ShapeDtypeStruct(exchange, BF16),
            jax.ShapeDtypeStruct((micro * criterion.shape[1], slots), F32),
        ],
        in_specs=spaces,
        out_specs=[
            pl.BlockSpec(memory_space=pl.ANY),
            pl.BlockSpec(memory_space=pltpu.VMEM),
        ],
        scratch_shapes=[
            pltpu.VMEM(w_value.shape, BF16),
            pltpu.VMEM(w_out.shape, BF16),
            pltpu.VMEM(w_out.shape, BF16),
            pltpu.VMEM(w_value.shape, BF16),
            pltpu.VMEM(down.shape, BF16),
            pltpu.VMEM(up.shape, BF16),
            row_buffer,
            row_buffer,
            row_buffer,
            row_buffer,
            row_buffer,
            pltpu.VMEM((rows, LANES), F32),
            pltpu.VMEM((rows, value_width), F32),
            pltpu.VMEM((rows, LANES), F32),
            pltpu.VMEM((rows, value_width), BF16),
            pltpu.VMEM((rows, LANES), BF16),
            pltpu.VMEM((rows, LANES), BF16),
            pltpu.VMEM(exchange, BF16),
            pltpu.VMEM(exchange, BF16),
            pltpu.VMEM((micro, width // 2, LANES), BF16),
            pltpu.VMEM((micro, value_width, LANES), BF16),
            pltpu.VMEM((value_width, LANES), F32),
            pltpu.VMEM(exchange, BF16),
            pltpu.SemaphoreType.DMA((4,)),
            pltpu.SemaphoreType.DMA((chunks, PIECES)),
            pltpu.SemaphoreType.DMA((chunks, PIECES)),
            pltpu.SemaphoreType.DMA((chunks, PIECES)),
            pltpu.SemaphoreType.DMA((chunks, PIECES)),
            pltpu.SemaphoreType.DMA((micro,)),
            pltpu.SemaphoreType.DMA((micro, peers)),
            pltpu.SemaphoreType.DMA((micro,)),
            pltpu.SemaphoreType.DMA((micro,)),
        ],
        compiler_params=pltpu.CompilerParams(
            collective_id=0, has_side_effects=True, vmem_limit_bytes=56 * 1024 * 1024
        ),
        name="chain",
    )(tokens, cotangent, gains, w_value, w_out, down, up, criterion, slot_of)


def place_kernel(picks, parts, down, up, chosen, held, down_out, up_out, pick_sem, load_sem, store_sem):
    pairs = parts.shape[0]
    groups = held.shape[0]
    up_half = up.shape[0] // 2
    half = down.shape[0] // 2
    pick_load = pltpu.make_async_copy(picks, chosen, pick_sem)
    pick_load.start()
    loads = [
        pltpu.make_async_copy(
            parts.at[:, pl.ds(index * GROUP, GROUP)], held.at[index], load_sem.at[index]
        )
        for index in range(groups)
    ]
    for load in loads:
        load.start()
    pick_load.wait()
    one = chosen[...].astype(BF16)
    none = jnp.zeros_like(one)
    pair_of = jnp.concatenate(
        [jnp.concatenate([one, none], axis=1), jnp.concatenate([none, one], axis=1)], axis=0
    )
    slots = chosen.shape[1]
    stores = []
    for index in range(0, groups, 2):
        span = min(2, groups - index)
        for load in loads[index : index + span]:
            load.wait()
        flat = jnp.concatenate([held[index + k] for k in range(span)], axis=0)
        flat = flat.reshape(span * pairs, GROUP * LANES)
        summed = dot_tn(flat, pair_of if span == 2 else one)
        for k in range(span):
            mine = summed[:, k * slots : (k + 1) * slots].reshape(GROUP, 2, LANES // 2, slots)
            for side in range(2):
                if index + k < groups - 1:
                    at = pl.ds(side * half + (index + k) * GROUP, GROUP)
                    source, target = down_out, down
                    down_out[at] = mine[:, side]
                else:
                    at = pl.ds(side * up_half, up_half)
                    source, target = up_out, up
                    up_out[at] = mine[0:up_half, side]
                store = pltpu.make_async_copy(
                    source.at[at], target.at[at], store_sem.at[index + k, side]
                )
                store.start()
                stores.append(store)
    for store in stores:
        store.wait()


def place(picks, parts, feature_rows, value_rows, rank):
    pairs, packed = parts.shape[0:2]
    slots = picks.shape[1]
    groups = packed // GROUP
    down_shape = (feature_rows, rank, slots)
    up_shape = (value_rows, rank, slots)
    return pl.pallas_call(
        place_kernel,
        in_specs=[pl.BlockSpec(memory_space=pltpu.HBM)] * 2,
        out_specs=[pl.BlockSpec(memory_space=pl.ANY)] * 2,
        out_shape=[
            jax.ShapeDtypeStruct(down_shape, F32),
            jax.ShapeDtypeStruct(up_shape, F32),
        ],
        scratch_shapes=[
            pltpu.VMEM((pairs, slots), F32),
            pltpu.VMEM((groups, pairs, GROUP, LANES), BF16),
            pltpu.VMEM(down_shape, F32),
            pltpu.VMEM(up_shape, F32),
            pltpu.SemaphoreType.DMA,
            pltpu.SemaphoreType.DMA((groups,)),
            pltpu.SemaphoreType.DMA((groups, 2)),
        ],
        compiler_params=pltpu.CompilerParams(vmem_limit_bytes=60 * 1024 * 1024),
        name="place",
    )(picks, parts)


def on_device(
    tokens,
    cotangent,
    norm_gain,
    value_weight,
    out_weight,
    adapter_down,
    adapter_up,
    criterion,
    slot_of,
):
    micro, block, width = tokens.shape
    down = jnp.transpose(adapter_down[0], (1, 2, 0))
    up = jnp.transpose(adapter_up[0], (1, 2, 0))
    parts, picks = run_chain(
        tokens.reshape(micro * block, width),
        cotangent.reshape(micro * block, width),
        norm_gain,
        value_weight[0],
        out_weight[0],
        down,
        up,
        criterion,
        slot_of,
    )
    parts = parts.reshape((parts.shape[0] * parts.shape[1],) + parts.shape[2:])
    grad_down, grad_up = place(picks, parts, down.shape[0], up.shape[0], down.shape[1])
    return (jnp.transpose(grad_down, (2, 0, 1))[None], jnp.transpose(grad_up, (2, 0, 1))[None])


def solution(mesh):
    return jax.shard_map(
        on_device,
        mesh=mesh,
        in_specs=(
            P(None, "dp", None),
            P(None, "dp", None),
            P("section", None),
            P("section", None, None),
            P("section", None, None),
            P("section", None, "dp", None),
            P("section", None, "dp", None),
            P(),
            P(),
        ),
        out_specs=(P("section", None, "dp", None), P("section", None, "dp", None)),
        check_vma=False,
    )
```

```python
import jax
import jax.numpy as jnp
from jax import lax
from jax.experimental import pallas as pl
from jax.experimental.pallas import tpu as pltpu
from jax.sharding import PartitionSpec as P

EPSILON = 1e-06
CHUNK = 16
TILE = 512
GROUP = 16
PIECES = 2
SENDS = 1
LANES = 128
BF16 = jnp.bfloat16
F32 = jnp.float32


def dot(left, right):
    return jnp.dot(left, right, preferred_element_type=F32)


def dot_nt(left, right):
    return lax.dot_general(left, right, (((1,), (1,)), ((), ())), preferred_element_type=F32)


def dot_tn(left, right):
    return lax.dot_general(left, right, (((0,), (0,)), ((), ())), preferred_element_type=F32)


def swap_halves(value):
    half = value.shape[-1] // 2
    return jnp.concatenate([value[:, half:], value[:, :half]], axis=1)


def fill_picks(picks, criterion, slot_of):
    micro, blocks = criterion.shape
    lanes = lax.broadcasted_iota(jnp.int32, (1, picks.shape[1]), 1)
    for index in range(micro * blocks):
        slot = slot_of[criterion[index // blocks, index % blocks]]
        picks[index : index + 1, :] = jnp.where(lanes == slot, 1.0, 0.0)


def chain_kernel(
    tokens,
    cotangent,
    gains_whole,
    w_value,
    w_out,
    down,
    up,
    criterion_whole,
    slot_of_whole,
    grad_recv,
    picks_out,
    gains,
    criterion,
    slot_of,
    picks,
    value_ref,
    out_ref,
    value_turned,
    out_turned,
    down_ref,
    up_ref,
    h_in,
    h_out,
    g_in,
    g_out,
    scaled,
    inverse,
    mixed_ref,
    narrow_ref,
    value_grad,
    low,
    low_grad,
    panel_send,
    panel_recv,
    panel_down,
    panel_up,
    product_up,
    grad_send,
    load_sem,
    down_sem,
    h_send_sem,
    h_recv_sem,
    g_send_sem,
    g_recv_sem,
    panel_send_sem,
    panel_recv_sem,
    grad_send_sem,
    grad_recv_sem,
):
    sections = lax.axis_size("section")
    peers = lax.axis_size("dp")
    section = lax.axis_index("section")
    me = lax.axis_index("dp")
    micro = criterion.shape[0]
    rows, width = h_in.shape
    block = rows // micro
    chunks = rows // CHUNK
    per_block = block // CHUNK
    slots = picks.shape[1]
    feature_rows = down.shape[0]
    value_rows = up.shape[0]
    down_half = feature_rows // 2
    up_half = value_rows // 2
    packed = panel_send.shape[2]
    value_width = value_grad.shape[1]
    piece_width = width // PIECES
    send_width = width // SENDS
    sends = [slice(start, start + send_width) for start in range(0, width, send_width)]
    first = section == 0
    last = section == sections - 1

    loads = [
        pltpu.make_async_copy(source, target, load_sem.at[place])
        for place, (source, target) in enumerate(
            [
                (criterion_whole, criterion),
                (slot_of_whole, slot_of),
                (up, up_ref),
                (gains_whole, gains),
                (w_value, value_ref),
                (w_out, out_ref),
                (picks, picks_out),
            ]
        )
    ]
    halves = [
        [
            pltpu.make_async_copy(
                down.at[pl.ds(side * down_half + start, GROUP)],
                down_ref.at[pl.ds(side * down_half + start, GROUP)],
                down_sem.at[side, start // GROUP],
            )
            for side in range(2)
        ]
        for start in range(0, down_half, GROUP)
    ]
    loads[0].start()
    loads[1].start()
    for both in halves:
        for load in both:
            load.start()
    loads[2].start()
    loads[3].start()

    def tiles_of(piece):
        base = piece * piece_width
        return [slice(base + at, base + at + TILE) for at in range(0, piece_width, TILE)]

    def chunk_rows(c):
        return pl.ds(pl.multiple_of(c * CHUNK, CHUNK), CHUNK)

    barrier = pltpu.get_barrier_semaphore()

    def greet(k, carry):
        pl.semaphore_signal(
            barrier,
            inc=1,
            device_id={"dp": lax.rem(me + k, peers)},
            device_id_type=pl.DeviceIdType.MESH,
        )
        return carry

    lax.fori_loop(1, peers, greet, 0)
    for step in (1, sections - 1):
        pl.semaphore_signal(
            barrier,
            inc=1,
            device_id={"section": lax.rem(section + step, sections)},
            device_id_type=pl.DeviceIdType.MESH,
        )

    loads[0].wait()
    loads[1].wait()
    fill_picks(picks, criterion, slot_of)
    loads[6].start()
    chosen = picks[...].astype(BF16)
    loads[4].start()

    loads[5].start()
    for start in range(0, down_half, GROUP):
        for load in halves[start // GROUP]:
            load.wait()
        pair = jnp.concatenate(
            [down_ref[start : start + GROUP], down_ref[down_half + start : down_half + start + GROUP]],
            axis=1,
        )
        found = dot_nt(chosen, pair.reshape(GROUP * LANES, slots))
        found = found.reshape(micro, peers, GROUP, LANES).astype(BF16)
        panel_send[:, :, start : start + GROUP, :] = found
    loads[2].wait()
    pair = jnp.concatenate([up_ref[0:up_half], up_ref[up_half:value_rows]], axis=1)
    found = dot_nt(chosen, pair.reshape(up_half * LANES, slots)).reshape(
        micro, peers, up_half, LANES
    )
    if packed - down_half > up_half:
        rest = jnp.zeros((micro, peers, packed - down_half - up_half, LANES), F32)
        found = jnp.concatenate([found, rest], axis=2)
    panel_send[:, :, down_half:packed, :] = found.astype(BF16)

    pl.semaphore_wait(barrier, peers + 1)

    def hand(m, peer, source, target, send_sem, landed):
        pltpu.make_async_remote_copy(
            src_ref=source.at[m, peer],
            dst_ref=target.at[m, me],
            send_sem=send_sem.at[m],
            recv_sem=landed,
            device_id={"dp": peer},
            device_id_type=pl.DeviceIdType.MESH,
        ).start()

    def keep(m, source, target, landed):
        pltpu.make_async_copy(source.at[m, me], target.at[m, me], landed).start()

    def spread_panels(m):
        landed = panel_recv_sem.at[m, me]

        def send(k, carry):
            peer = lax.rem(me + k // 2 + k % 2 * (peers // 2), peers)
            hand(m, peer, panel_send, panel_recv, panel_send_sem, landed)
            return carry

        keep(m, panel_send, panel_recv, landed)
        lax.fori_loop(1, peers, send, 0)

    def wait_for(ref, sem):
        pltpu.make_async_copy(ref, ref, sem).wait()

    spread_panels(0)

    @pl.when(first)
    def _():
        for c in range(chunks):
            part = pl.ds(c * CHUNK, CHUNK)
            for piece in range(SENDS):
                pltpu.make_async_copy(
                    tokens.at[part, sends[piece]],
                    h_in.at[part, sends[piece]],
                    h_recv_sem.at[c, piece],
                ).start()

    @pl.when(last)
    def _():
        for c in range(chunks):
            part = pl.ds(c * CHUNK, CHUNK)
            for piece in range(SENDS):
                pltpu.make_async_copy(
                    cotangent.at[part, sends[piece]],
                    g_in.at[part, sends[piece]],
                    g_recv_sem.at[c, piece],
                ).start()

    loads[3].wait()
    loads[4].wait()

    near = lax.broadcasted_iota(jnp.int32, (down_half, LANES), 1) < LANES // 2
    near_up = near[0:up_half]
    near_row = near[0:CHUNK]

    def unpack(m):
        def one(k, carry):
            source = lax.rem(me - k + peers, peers // 2)
            for place in (source, source + peers // 2):
                wait_for(panel_recv.at[m, place], panel_recv_sem.at[m, place])
            at = pl.multiple_of(source * feature_rows, 2 * GROUP)
            part = panel_recv[m, source, 0:down_half, :]
            other = panel_recv[m, source + peers // 2, 0:down_half, :]
            crossed = swap_halves(jnp.where(near, other, part))
            panel_down[m, pl.ds(at, down_half), :] = jnp.where(near, part, crossed)
            panel_down[m, pl.ds(at + down_half, down_half), :] = jnp.where(near, crossed, other)
            for place in (source, source + peers // 2):
                at = pl.multiple_of(place * value_rows, GROUP)
                part = panel_recv[m, place, down_half:packed, :].astype(F32)[0:up_half]
                both = [jnp.where(near_up, part, 0.0), jnp.where(near_up, 0.0, part)]
                panel_up[m, pl.ds(at, value_rows), :] = jnp.concatenate(both, axis=0).astype(BF16)
            return carry

        lax.fori_loop(0, peers // 2, one, 0)

        @pl.when((section > 0) & (m < micro - 1))
        def _():
            spread_panels(m + 1)

    def wait_piece(ref, sem, c, piece):
        for index in range(SENDS) if piece == 0 else []:
            wait_for(ref.at[chunk_rows(c), sends[index]], sem.at[c, index])

    def send_piece(source, target, c, piece, send_sem, recv_sem, to):
        here = chunk_rows(c)
        columns = sends[piece]
        pltpu.make_async_remote_copy(
            src_ref=source.at[here, columns],
            dst_ref=target.at[here, columns],
            send_sem=send_sem.at[c, piece],
            recv_sem=recv_sem.at[c, piece],
            device_id={"section": to},
            device_id_type=pl.DeviceIdType.MESH,
        ).start()

    def forward(c):
        m = c // per_block
        here = chunk_rows(c)

        @pl.when(first & (c % per_block == 0))
        def _():
            unpack(m)

        squares = jnp.zeros((CHUNK, LANES), F32)
        mixed = jnp.zeros((CHUNK, value_width), F32)
        narrow = jnp.zeros((2 * CHUNK, LANES), F32)
        for piece in range(PIECES):
            wait_piece(h_in, h_recv_sem, c, piece)
            for tile in tiles_of(piece):
                hidden = h_in[here, tile].astype(F32)
                square = hidden * hidden
                for start in range(0, TILE, LANES):
                    squares += square[:, start : start + LANES]
                scaled[here, tile] = (hidden * gains[:, tile]).astype(BF16)
            if piece == PIECES - 1:
                for tile, far in zip(tiles_of(0), tiles_of(1)):
                    both = jnp.concatenate([scaled[here, tile], scaled[here, far]], axis=0)
                    narrow += dot(both, panel_down[m, tile, :])
            for tile in tiles_of(piece):
                mixed += dot(scaled[here, tile], value_ref[tile, :])
        total = jnp.sum(squares, axis=1, keepdims=True)
        factor = lax.rsqrt(total / width + EPSILON)
        inverse[here, :] = jnp.broadcast_to(factor, (CHUNK, LANES))
        mixed_ref[here, :] = mixed
        narrow = jnp.where(near_row, narrow[0:CHUNK], narrow[CHUNK : 2 * CHUNK])
        narrow_ref[here, :] = narrow
        narrow = ((narrow + swap_halves(narrow)) * factor).astype(BF16)
        low[here, :] = narrow
        values = (mixed * factor + dot_nt(narrow, panel_up[m])).astype(BF16)

        @pl.when(section < sections - 1)
        def _():
            for piece in range(PIECES):
                for tile in tiles_of(piece):
                    added = dot(values, out_ref[:, tile])
                    h_out[here, tile] = (h_in[here, tile].astype(F32) + added).astype(BF16)
                    if tile.stop % send_width == 0:
                        done = tile.stop // send_width - 1
                        send_piece(h_out, h_in, c, done, h_send_sem, h_recv_sem, section + 1)

    def pull(c, carry):
        here = chunk_rows(c)
        pulled = jnp.zeros((CHUNK, value_width), F32)
        for piece in range(PIECES):
            wait_piece(g_in, g_recv_sem, c, piece)
            for tile in tiles_of(piece):
                pulled += dot(g_in[here, tile], out_turned[tile, :])
        value_grad[here, :] = pulled.astype(BF16)
        return carry

    def lower(c, pulled):
        here = chunk_rows(c)
        narrow = dot(pulled, panel_up[c // per_block])
        narrow = narrow + swap_halves(narrow)
        factor = inverse[here, 0:1]
        low_grad[here, :] = (narrow * factor).astype(BF16)
        return narrow.astype(BF16), factor

    def backward(c):
        m = c // per_block
        here = chunk_rows(c)

        @pl.when(first)
        def _():
            lower(c, value_grad[here, :])

        @pl.when(section > 0)
        def _():
            pulled = value_grad[here, :]
            held, factor = lower(c, pulled)
            parts = [dot(pulled, value_turned[:, tile]) for tile in tiles_of(0)]
            along = pulled.astype(F32) * mixed_ref[here, :]
            moment = jnp.sum(along, axis=1, keepdims=True)
            along = held.astype(F32) * narrow_ref[here, :]
            moment += jnp.sum(along, axis=1, keepdims=True)
            bend = factor * factor * factor * (moment / width)
            none = jnp.zeros_like(held)
            both = [jnp.where(near_row, held, none), jnp.where(near_row, none, held)]
            both = jnp.concatenate(both, axis=0)
            lifts = [dot_nt(both, panel_down[m, tile, :]) for tile in tiles_of(0)]
            for piece in range(PIECES):
                if piece > 0:
                    parts = [dot(pulled, value_turned[:, tile]) for tile in tiles_of(piece)]
                for part, lift, tile in zip(parts, lifts, tiles_of(piece)):
                    part += lift[piece * CHUNK : (piece + 1) * CHUNK]
                    result = (
                        g_in[here, tile].astype(F32)
                        + factor * (part * gains[:, tile])
                        - h_in[here, tile].astype(F32) * bend
                    )
                    g_out[here, tile] = result.astype(BF16)
                    if tile.stop % send_width == 0:
                        done = tile.stop // send_width - 1
                        send_piece(g_out, g_in, c, done, g_send_sem, g_recv_sem, section - 1)

    def products(m):
        here = pl.ds(pl.multiple_of(m * block, block), block)
        product_up[...] = dot_tn(value_grad[here, :], low[here, :])
        several = min(4, peers)
        span = several * feature_rows

        def group(k, carry):
            which = lax.rem(me // several + k, peers // several)
            columns = pl.ds(pl.multiple_of(which * span, LANES), span)
            product = dot_tn(scaled[here, columns], low_grad[here, :]).astype(BF16)
            for q in range(several):
                peer = which * several + q
                at = q * feature_rows
                part = product[at : at + down_half]
                other = product[at + down_half : at + feature_rows]
                grad_send[m, peer, 0:down_half, :] = jnp.where(near, part, other)
                at = pl.multiple_of(peer * value_rows, GROUP)
                part = product_up[pl.ds(at, value_rows), :]
                part = jnp.where(near_up, part[0:up_half], part[up_half:value_rows])
                if packed - down_half > up_half:
                    rest = jnp.zeros((packed - down_half - up_half, LANES), F32)
                    part = jnp.concatenate([part, rest], axis=0)
                grad_send[m, peer, down_half:packed, :] = part.astype(BF16)

                @pl.when(peer != me)
                def _():
                    hand(m, peer, grad_send, grad_recv, grad_send_sem, grad_recv_sem.at[m])

                @pl.when(peer == me)
                def _():
                    keep(m, grad_send, grad_recv, grad_recv_sem.at[m])

            return carry

        lax.fori_loop(0, peers // several, group, 0)

    def turn():
        def one(index, carry):
            at = pl.ds(pl.multiple_of(index * TILE, TILE), TILE)
            out_turned[at, :] = out_ref[:, at].T
            value_turned[:, at] = value_ref[at, :].T
            return carry

        lax.fori_loop(0, width // TILE, one, 0)

    lag = jnp.where(first, chunks, jnp.where(last, 0, (sections - 1 - section) * 3 + (2 - section)))
    lag = jnp.minimum(lag, chunks)

    loads[5].wait()
    turn_at = jnp.where(first, chunks, 0)

    drawn = jnp.minimum(jnp.maximum(lag + per_block, chunks + 1), chunks + lag) - 1

    def step(t, carry):
        @pl.when(t == turn_at)
        def _():
            turn()
            lax.fori_loop(0, jnp.where(last, chunks, 0), pull, 0)

        @pl.when((section > 0) & ((t == 0) | (t == per_block // 2)))
        def _():
            unpack(jnp.where(t == 0, 0, 1))

        @pl.when(first & (t == per_block // 2 - 1))
        def _():
            spread_panels(1)

        @pl.when(t < chunks)
        def _():
            forward(t)

        c = t - lag

        @pl.when((c >= 0) & (c < chunks))
        def _():
            @pl.when(section < sections - 1)
            def _():
                pull(c, 0)

            backward(c)

        @pl.when(t == drawn)
        def _():
            products(0)

        @pl.when(t == chunks + lag - 1)
        def _():
            products(1)

        return carry

    lax.fori_loop(0, chunks + lag, step, 0)

    loads[6].wait()

    for m in range(micro):
        wait_for(grad_recv.at[m], grad_recv_sem.at[m])
        for source, sem in ((panel_send, panel_send_sem), (grad_send, grad_send_sem)):
            wait_for(source.at[m, 0 : peers - 1], sem.at[m])

    @pl.when(section < sections - 1)
    def _():
        for c in range(chunks):
            for piece in range(SENDS):
                part = h_out.at[pl.ds(c * CHUNK, CHUNK), sends[piece]]
                wait_for(part, h_send_sem.at[c, piece])

    @pl.when(section > 0)
    def _():
        for c in range(chunks):
            for piece in range(SENDS):
                part = g_out.at[pl.ds(c * CHUNK, CHUNK), sends[piece]]
                wait_for(part, g_send_sem.at[c, piece])


def run_chain(tokens, cotangent, gains, w_value, w_out, down, up, criterion, slot_of):
    micro = criterion.shape[0]
    peers = lax.axis_size("dp")
    rows, width = tokens.shape
    value_width = w_out.shape[0]
    chunks = rows // CHUNK
    slots = down.shape[2]
    useful = (down.shape[0] + up.shape[0]) // 2
    packed = (useful + 15) // 16 * 16
    block = rows // micro
    spaces = [pl.BlockSpec(memory_space=pl.ANY)] * 9
    row_buffer = pltpu.VMEM((rows, width), BF16)
    exchange = (micro, peers, packed, LANES)
    return pl.pallas_call(
        chain_kernel,
        out_shape=[
            jax.ShapeDtypeStruct(exchange, BF16),
            jax.ShapeDtypeStruct((micro * criterion.shape[1], slots), F32),
        ],
        in_specs=spaces,
        out_specs=[pl.BlockSpec(memory_space=pl.ANY)] * 2,
        scratch_shapes=[
            pltpu.VMEM(gains.shape, F32),
            pltpu.SMEM(criterion.shape, jnp.int32),
            pltpu.SMEM(slot_of.shape, jnp.int32),
            pltpu.VMEM((micro * criterion.shape[1], slots), F32),
            pltpu.VMEM(w_value.shape, BF16),
            pltpu.VMEM(w_out.shape, BF16),
            pltpu.VMEM(w_out.shape, BF16),
            pltpu.VMEM(w_value.shape, BF16),
            pltpu.VMEM(down.shape, BF16),
            pltpu.VMEM(up.shape, BF16),
            row_buffer,
            row_buffer,
            row_buffer,
            row_buffer,
            row_buffer,
            pltpu.VMEM((rows, LANES), F32),
            pltpu.VMEM((rows, value_width), F32),
            pltpu.VMEM((rows, LANES), F32),
            pltpu.VMEM((rows, value_width), BF16),
            pltpu.VMEM((rows, LANES), BF16),
            pltpu.VMEM((rows, LANES), BF16),
            pltpu.VMEM(exchange, BF16),
            pltpu.VMEM(exchange, BF16),
            pltpu.VMEM((micro, width // 2, LANES), BF16),
            pltpu.VMEM((micro, value_width, LANES), BF16),
            pltpu.VMEM((value_width, LANES), F32),
            pltpu.VMEM(exchange, BF16),
            pltpu.SemaphoreType.DMA((7,)),
            pltpu.SemaphoreType.DMA((2, down.shape[0] // 2 // GROUP)),
            pltpu.SemaphoreType.DMA((chunks, SENDS)),
            pltpu.SemaphoreType.DMA((chunks, SENDS)),
            pltpu.SemaphoreType.DMA((chunks, SENDS)),
            pltpu.SemaphoreType.DMA((chunks, SENDS)),
            pltpu.SemaphoreType.DMA((micro,)),
            pltpu.SemaphoreType.DMA((micro, peers)),
            pltpu.SemaphoreType.DMA((micro,)),
            pltpu.SemaphoreType.DMA((micro,)),
        ],
        compiler_params=pltpu.CompilerParams(
            collective_id=0, has_side_effects=True, vmem_limit_bytes=56 * 1024 * 1024
        ),
        name="chain",
    )(tokens, cotangent, gains, w_value, w_out, down, up, criterion, slot_of)


def place_kernel(picks, parts, down, up, chosen, held, down_out, up_out, pick_sem, load_sem, store_sem):
    pairs = parts.shape[0]
    groups = held.shape[0]
    up_half = up.shape[0] // 2
    half = down.shape[0] // 2
    pick_load = pltpu.make_async_copy(picks, chosen, pick_sem)
    pick_load.start()
    loads = [
        pltpu.make_async_copy(
            parts.at[:, pl.ds(index * GROUP, GROUP)], held.at[index], load_sem.at[index]
        )
        for index in range(groups)
    ]
    for load in loads:
        load.start()
    pick_load.wait()
    one = chosen[...].astype(BF16)
    none = jnp.zeros_like(one)
    pair_of = jnp.concatenate(
        [jnp.concatenate([one, none], axis=1), jnp.concatenate([none, one], axis=1)], axis=0
    )
    slots = chosen.shape[1]
    stores = []
    for index in range(0, groups, 2):
        span = min(2, groups - index)
        for load in loads[index : index + span]:
            load.wait()
        flat = jnp.concatenate([held[index + k] for k in range(span)], axis=0)
        flat = flat.reshape(span * pairs, GROUP * LANES)
        summed = dot_tn(flat, pair_of if span == 2 else one)
        for k in range(span):
            mine = summed[:, k * slots : (k + 1) * slots].reshape(GROUP, 2, LANES // 2, slots)
            for side in range(2):
                if index + k < groups - 1:
                    at = pl.ds(side * half + (index + k) * GROUP, GROUP)
                    source, target = down_out, down
                    down_out[at] = mine[:, side]
                else:
                    at = pl.ds(side * up_half, up_half)
                    source, target = up_out, up
                    up_out[at] = mine[0:up_half, side]
                store = pltpu.make_async_copy(
                    source.at[at], target.at[at], store_sem.at[index + k, side]
                )
                store.start()
                stores.append(store)
    for store in stores:
        store.wait()


def place(picks, parts, feature_rows, value_rows, rank):
    pairs, packed = parts.shape[0:2]
    slots = picks.shape[1]
    groups = packed // GROUP
    down_shape = (feature_rows, rank, slots)
    up_shape = (value_rows, rank, slots)
    return pl.pallas_call(
        place_kernel,
        in_specs=[pl.BlockSpec(memory_space=pltpu.HBM)] * 2,
        out_specs=[pl.BlockSpec(memory_space=pl.ANY)] * 2,
        out_shape=[
            jax.ShapeDtypeStruct(down_shape, F32),
            jax.ShapeDtypeStruct(up_shape, F32),
        ],
        scratch_shapes=[
            pltpu.VMEM((pairs, slots), F32),
            pltpu.VMEM((groups, pairs, GROUP, LANES), BF16),
            pltpu.VMEM(down_shape, F32),
            pltpu.VMEM(up_shape, F32),
            pltpu.SemaphoreType.DMA,
            pltpu.SemaphoreType.DMA((groups,)),
            pltpu.SemaphoreType.DMA((groups, 2)),
        ],
        compiler_params=pltpu.CompilerParams(vmem_limit_bytes=60 * 1024 * 1024),
        name="place",
    )(picks, parts)


def on_device(
    tokens,
    cotangent,
    norm_gain,
    value_weight,
    out_weight,
    adapter_down,
    adapter_up,
    criterion,
    slot_of,
):
    micro, block, width = tokens.shape
    down = jnp.transpose(adapter_down[0], (1, 2, 0))
    up = jnp.transpose(adapter_up[0], (1, 2, 0))
    parts, picks = run_chain(
        tokens.reshape(micro * block, width),
        cotangent.reshape(micro * block, width),
        norm_gain,
        value_weight[0],
        out_weight[0],
        down,
        up,
        criterion,
        slot_of,
    )
    parts = parts.reshape((parts.shape[0] * parts.shape[1],) + parts.shape[2:])
    grad_down, grad_up = place(picks, parts, down.shape[0], up.shape[0], down.shape[1])
    return (jnp.transpose(grad_down, (2, 0, 1))[None], jnp.transpose(grad_up, (2, 0, 1))[None])


def solution(mesh):
    return jax.shard_map(
        on_device,
        mesh=mesh,
        in_specs=(
            P(None, "dp", None),
            P(None, "dp", None),
            P("section", None),
            P("section", None, None),
            P("section", None, None),
            P("section", None, "dp", None),
            P("section", None, "dp", None),
            P(),
            P(),
        ),
        out_specs=(P("section", None, "dp", None), P("section", None, "dp", None)),
        check_vma=False,
    )
```

```python
import jax
import jax.numpy as jnp
from jax import lax
from jax.experimental import pallas as pl
from jax.experimental.pallas import tpu as pltpu
from jax.sharding import PartitionSpec as P

EPSILON = 1e-06
CHUNK = 16
TILE = 512
GROUP = 16
PIECES = 2
SENDS = 1
LANES = 128
BF16 = jnp.bfloat16
F32 = jnp.float32


def dot(left, right):
    return jnp.dot(left, right, preferred_element_type=F32)


def dot_nt(left, right):
    return lax.dot_general(left, right, (((1,), (1,)), ((), ())), preferred_element_type=F32)


def dot_tn(left, right):
    return lax.dot_general(left, right, (((0,), (0,)), ((), ())), preferred_element_type=F32)


def swap_halves(value):
    half = value.shape[-1] // 2
    return jnp.concatenate([value[:, half:], value[:, :half]], axis=1)


def fill_picks(picks, criterion, slot_of):
    micro, blocks = criterion.shape
    lanes = lax.broadcasted_iota(jnp.int32, (1, picks.shape[1]), 1)
    for index in range(micro * blocks):
        slot = slot_of[criterion[index // blocks, index % blocks]]
        picks[index : index + 1, :] = jnp.where(lanes == slot, 1.0, 0.0)


def chain_kernel(
    tokens,
    cotangent,
    gains_whole,
    w_value,
    w_out,
    down,
    up,
    criterion_whole,
    slot_of_whole,
    grad_recv,
    picks_out,
    gains,
    criterion,
    slot_of,
    picks,
    value_ref,
    out_ref,
    value_turned,
    out_turned,
    down_ref,
    up_ref,
    h_in,
    h_out,
    g_in,
    g_out,
    scaled,
    inverse,
    mixed_ref,
    narrow_ref,
    value_grad,
    low,
    low_grad,
    panel_send,
    panel_recv,
    panel_down,
    panel_up,
    product_up,
    grad_send,
    load_sem,
    down_sem,
    h_send_sem,
    h_recv_sem,
    g_send_sem,
    g_recv_sem,
    panel_send_sem,
    panel_recv_sem,
    grad_send_sem,
    grad_recv_sem,
):
    sections = lax.axis_size("section")
    peers = lax.axis_size("dp")
    section = lax.axis_index("section")
    me = lax.axis_index("dp")
    micro = criterion.shape[0]
    rows, width = h_in.shape
    block = rows // micro
    chunks = rows // CHUNK
    per_block = block // CHUNK
    slots = picks.shape[1]
    feature_rows = down.shape[0]
    value_rows = up.shape[0]
    down_half = feature_rows // 2
    up_half = value_rows // 2
    packed = panel_send.shape[2]
    value_width = value_grad.shape[1]
    piece_width = width // PIECES
    send_width = width // SENDS
    sends = [slice(start, start + send_width) for start in range(0, width, send_width)]
    first = section == 0
    last = section == sections - 1

    loads = [
        pltpu.make_async_copy(source, target, load_sem.at[place])
        for place, (source, target) in enumerate(
            [
                (criterion_whole, criterion),
                (slot_of_whole, slot_of),
                (up, up_ref),
                (gains_whole, gains),
                (w_value, value_ref),
                (w_out, out_ref),
                (picks, picks_out),
            ]
        )
    ]
    halves = [
        [
            pltpu.make_async_copy(
                down.at[pl.ds(side * down_half + start, GROUP)],
                down_ref.at[pl.ds(side * down_half + start, GROUP)],
                down_sem.at[side, start // GROUP],
            )
            for side in range(2)
        ]
        for start in range(0, down_half, GROUP)
    ]
    loads[0].start()
    loads[1].start()
    for both in halves:
        for load in both:
            load.start()
    loads[2].start()
    loads[3].start()

    def tiles_of(piece):
        base = piece * piece_width
        return [slice(base + at, base + at + TILE) for at in range(0, piece_width, TILE)]

    def chunk_rows(c):
        return pl.ds(pl.multiple_of(c * CHUNK, CHUNK), CHUNK)

    barrier = pltpu.get_barrier_semaphore()

    def greet(k, carry):
        pl.semaphore_signal(
            barrier,
            inc=1,
            device_id={"dp": lax.rem(me + k, peers)},
            device_id_type=pl.DeviceIdType.MESH,
        )
        return carry

    lax.fori_loop(1, peers, greet, 0)
    for step in (1, sections - 1):
        pl.semaphore_signal(
            barrier,
            inc=1,
            device_id={"section": lax.rem(section + step, sections)},
            device_id_type=pl.DeviceIdType.MESH,
        )

    loads[0].wait()
    loads[1].wait()
    fill_picks(picks, criterion, slot_of)
    loads[6].start()
    chosen = picks[...].astype(BF16)
    loads[4].start()

    loads[5].start()
    for start in range(0, down_half, GROUP):
        for load in halves[start // GROUP]:
            load.wait()
        pair = jnp.concatenate(
            [down_ref[start : start + GROUP], down_ref[down_half + start : down_half + start + GROUP]],
            axis=1,
        )
        found = dot_nt(chosen, pair.reshape(GROUP * LANES, slots))
        found = found.reshape(micro, peers, GROUP, LANES).astype(BF16)
        panel_send[:, :, start : start + GROUP, :] = found
    loads[2].wait()
    pair = jnp.concatenate([up_ref[0:up_half], up_ref[up_half:value_rows]], axis=1)
    found = dot_nt(chosen, pair.reshape(up_half * LANES, slots)).reshape(
        micro, peers, up_half, LANES
    )
    if packed - down_half > up_half:
        rest = jnp.zeros((micro, peers, packed - down_half - up_half, LANES), F32)
        found = jnp.concatenate([found, rest], axis=2)
    panel_send[:, :, down_half:packed, :] = found.astype(BF16)

    pl.semaphore_wait(barrier, peers + 1)

    def hand(m, peer, source, target, send_sem, landed):
        pltpu.make_async_remote_copy(
            src_ref=source.at[m, peer],
            dst_ref=target.at[m, me],
            send_sem=send_sem.at[m],
            recv_sem=landed,
            device_id={"dp": peer},
            device_id_type=pl.DeviceIdType.MESH,
        ).start()

    def keep(m, source, target, landed):
        pltpu.make_async_copy(source.at[m, me], target.at[m, me], landed).start()

    def spread_panels(m):
        landed = panel_recv_sem.at[m, me]

        def send(k, carry):
            peer = lax.rem(me + k // 2 + k % 2 * (peers // 2), peers)
            hand(m, peer, panel_send, panel_recv, panel_send_sem, landed)
            return carry

        keep(m, panel_send, panel_recv, landed)
        lax.fori_loop(1, peers, send, 0)

    def wait_for(ref, sem):
        pltpu.make_async_copy(ref, ref, sem).wait()

    spread_panels(0)

    @pl.when(first)
    def _():
        for c in range(chunks):
            part = pl.ds(c * CHUNK, CHUNK)
            for piece in range(SENDS):
                pltpu.make_async_copy(
                    tokens.at[part, sends[piece]],
                    h_in.at[part, sends[piece]],
                    h_recv_sem.at[c, piece],
                ).start()

    @pl.when(last)
    def _():
        for c in range(chunks):
            part = pl.ds(c * CHUNK, CHUNK)
            for piece in range(SENDS):
                pltpu.make_async_copy(
                    cotangent.at[part, sends[piece]],
                    g_in.at[part, sends[piece]],
                    g_recv_sem.at[c, piece],
                ).start()

    loads[3].wait()
    loads[4].wait()

    near = lax.broadcasted_iota(jnp.int32, (down_half, LANES), 1) < LANES // 2
    near_up = near[0:up_half]
    near_row = near[0:CHUNK]

    def unpack(m):
        def one(k, carry):
            source = lax.rem(me - k + peers, peers // 2)
            for place in (source, source + peers // 2):
                wait_for(panel_recv.at[m, place], panel_recv_sem.at[m, place])
            at = pl.multiple_of(source * feature_rows, 2 * GROUP)
            part = panel_recv[m, source, 0:down_half, :]
            other = panel_recv[m, source + peers // 2, 0:down_half, :]
            crossed = swap_halves(jnp.where(near, other, part))
            panel_down[m, pl.ds(at, down_half), :] = jnp.where(near, part, crossed)
            panel_down[m, pl.ds(at + down_half, down_half), :] = jnp.where(near, crossed, other)
            for place in (source, source + peers // 2):
                at = pl.multiple_of(place * value_rows, GROUP)
                part = panel_recv[m, place, down_half:packed, :].astype(F32)[0:up_half]
                both = [jnp.where(near_up, part, 0.0), jnp.where(near_up, 0.0, part)]
                panel_up[m, pl.ds(at, value_rows), :] = jnp.concatenate(both, axis=0).astype(BF16)
            return carry

        lax.fori_loop(0, peers // 2, one, 0)

        @pl.when((section > 0) & (m < micro - 1))
        def _():
            spread_panels(m + 1)

    def wait_piece(ref, sem, c, piece):
        for index in range(SENDS) if piece == 0 else []:
            wait_for(ref.at[chunk_rows(c), sends[index]], sem.at[c, index])

    def send_piece(source, target, c, piece, send_sem, recv_sem, to):
        here = chunk_rows(c)
        columns = sends[piece]
        pltpu.make_async_remote_copy(
            src_ref=source.at[here, columns],
            dst_ref=target.at[here, columns],
            send_sem=send_sem.at[c, piece],
            recv_sem=recv_sem.at[c, piece],
            device_id={"section": to},
            device_id_type=pl.DeviceIdType.MESH,
        ).start()

    def forward(c, onward):
        m = c // per_block
        here = chunk_rows(c)

        @pl.when(first & (c % per_block == 0))
        def _():
            unpack(m)

        squares = jnp.zeros((CHUNK, LANES), F32)
        mixed = jnp.zeros((CHUNK, value_width), F32)
        narrow = jnp.zeros((2 * CHUNK, LANES), F32)
        for piece in range(PIECES):
            wait_piece(h_in, h_recv_sem, c, piece)
            for tile in tiles_of(piece):
                hidden = h_in[here, tile].astype(F32)
                square = hidden * hidden
                for start in range(0, TILE, LANES):
                    squares += square[:, start : start + LANES]
                scaled[here, tile] = (hidden * gains[:, tile]).astype(BF16)
            if piece == PIECES - 1:
                for tile, far in zip(tiles_of(0), tiles_of(1)):
                    both = jnp.concatenate([scaled[here, tile], scaled[here, far]], axis=0)
                    narrow += dot(both, panel_down[m, tile, :])
            for tile in tiles_of(piece):
                mixed += dot(scaled[here, tile], value_ref[tile, :])
        total = jnp.sum(squares, axis=1, keepdims=True)
        factor = lax.rsqrt(total / width + EPSILON)
        inverse[here, :] = jnp.broadcast_to(factor, (CHUNK, LANES))
        mixed_ref[here, :] = mixed
        narrow = jnp.where(near_row, narrow[0:CHUNK], narrow[CHUNK : 2 * CHUNK])
        narrow_ref[here, :] = narrow
        narrow = ((narrow + swap_halves(narrow)) * factor).astype(BF16)
        low[here, :] = narrow
        values = (mixed * factor + dot_nt(narrow, panel_up[m])).astype(BF16)

        if onward:
            for piece in range(PIECES):
                for tile in tiles_of(piece):
                    added = dot(values, out_ref[:, tile])
                    h_out[here, tile] = (h_in[here, tile].astype(F32) + added).astype(BF16)
                    if tile.stop % send_width == 0:
                        done = tile.stop // send_width - 1
                        send_piece(h_out, h_in, c, done, h_send_sem, h_recv_sem, section + 1)

    def pull(c, carry):
        here = chunk_rows(c)
        pulled = jnp.zeros((CHUNK, value_width), F32)
        for piece in range(PIECES):
            wait_piece(g_in, g_recv_sem, c, piece)
            for tile in tiles_of(piece):
                pulled += dot(g_in[here, tile], out_turned[tile, :])
        value_grad[here, :] = pulled.astype(BF16)
        return carry

    def lower(c, pulled):
        here = chunk_rows(c)
        narrow = dot(pulled, panel_up[c // per_block])
        narrow = narrow + swap_halves(narrow)
        factor = inverse[here, 0:1]
        low_grad[here, :] = (narrow * factor).astype(BF16)
        return narrow.astype(BF16), factor

    def backward(c, drawn_before, onward):
        here = chunk_rows(c)
        if not drawn_before:
            pull(c, 0)
        pulled = value_grad[here, :]
        if not onward:
            lower(c, pulled)
            return
        m = c // per_block
        held, factor = lower(c, pulled)
        parts = [dot(pulled, value_turned[:, tile]) for tile in tiles_of(0)]
        along = pulled.astype(F32) * mixed_ref[here, :]
        moment = jnp.sum(along, axis=1, keepdims=True)
        along = held.astype(F32) * narrow_ref[here, :]
        moment += jnp.sum(along, axis=1, keepdims=True)
        bend = factor * factor * factor * (moment / width)
        none = jnp.zeros_like(held)
        both = [jnp.where(near_row, held, none), jnp.where(near_row, none, held)]
        both = jnp.concatenate(both, axis=0)
        lifts = [dot_nt(both, panel_down[m, tile, :]) for tile in tiles_of(0)]
        for piece in range(PIECES):
            if piece > 0:
                parts = [dot(pulled, value_turned[:, tile]) for tile in tiles_of(piece)]
            for part, lift, tile in zip(parts, lifts, tiles_of(piece)):
                part += lift[piece * CHUNK : (piece + 1) * CHUNK]
                result = (
                    g_in[here, tile].astype(F32)
                    + factor * (part * gains[:, tile])
                    - h_in[here, tile].astype(F32) * bend
                )
                g_out[here, tile] = result.astype(BF16)
                if tile.stop % send_width == 0:
                    done = tile.stop // send_width - 1
                    send_piece(g_out, g_in, c, done, g_send_sem, g_recv_sem, section - 1)

    def products(m):
        here = pl.ds(pl.multiple_of(m * block, block), block)
        product_up[...] = dot_tn(value_grad[here, :], low[here, :])
        several = min(4, peers)
        span = several * feature_rows

        def group(k, carry):
            which = lax.rem(me // several + k, peers // several)
            columns = pl.ds(pl.multiple_of(which * span, LANES), span)
            product = dot_tn(scaled[here, columns], low_grad[here, :]).astype(BF16)
            for q in range(several):
                peer = which * several + q
                at = q * feature_rows
                part = product[at : at + down_half]
                other = product[at + down_half : at + feature_rows]
                grad_send[m, peer, 0:down_half, :] = jnp.where(near, part, other)
                at = pl.multiple_of(peer * value_rows, GROUP)
                part = product_up[pl.ds(at, value_rows), :]
                part = jnp.where(near_up, part[0:up_half], part[up_half:value_rows])
                if packed - down_half > up_half:
                    rest = jnp.zeros((packed - down_half - up_half, LANES), F32)
                    part = jnp.concatenate([part, rest], axis=0)
                grad_send[m, peer, down_half:packed, :] = part.astype(BF16)

                @pl.when(peer != me)
                def _():
                    hand(m, peer, grad_send, grad_recv, grad_send_sem, grad_recv_sem.at[m])

                @pl.when(peer == me)
                def _():
                    keep(m, grad_send, grad_recv, grad_recv_sem.at[m])

            return carry

        lax.fori_loop(0, peers // several, group, 0)

    def turn():
        def one(index, carry):
            at = pl.ds(pl.multiple_of(index * TILE, TILE), TILE)
            out_turned[at, :] = out_ref[:, at].T
            value_turned[:, at] = value_ref[at, :].T
            return carry

        lax.fori_loop(0, width // TILE, one, 0)

    lag = jnp.where(first, chunks, jnp.where(last, 0, (sections - 1 - section) * 3 + (2 - section)))
    lag = jnp.minimum(lag, chunks)

    loads[5].wait()
    turn_at = jnp.where(first, chunks, 0)

    drawn = jnp.minimum(jnp.maximum(lag + per_block, chunks + 1), chunks + lag) - 1

    def step(t, carry):
        @pl.when(t == turn_at)
        def _():
            turn()
            lax.fori_loop(0, jnp.where(last, chunks, 0), pull, 0)

        @pl.when((section > 0) & ((t == 0) | (t == per_block // 2)))
        def _():
            unpack(jnp.where(t == 0, 0, 1))

        @pl.when(first & (t == per_block // 2 - 1))
        def _():
            spread_panels(1)

        @pl.when((t < chunks) & (section < sections - 1))
        def _():
            forward(t, True)

        @pl.when((t < chunks) & last)
        def _():
            forward(t, False)

        c = t - lag

        live = (c >= 0) & (c < chunks)

        @pl.when(live & first)
        def _():
            backward(c, False, False)

        @pl.when(live & (section > 0) & (section < sections - 1))
        def _():
            backward(c, False, True)

        @pl.when(live & last)
        def _():
            backward(c, True, True)

        @pl.when(t == drawn)
        def _():
            products(0)

        @pl.when(t == chunks + lag - 1)
        def _():
            products(1)

        return carry

    lax.fori_loop(0, chunks + lag, step, 0)

    loads[6].wait()

    for m in range(micro):
        wait_for(grad_recv.at[m], grad_recv_sem.at[m])
        for source, sem in ((panel_send, panel_send_sem), (grad_send, grad_send_sem)):
            wait_for(source.at[m, 0 : peers - 1], sem.at[m])

    @pl.when(section < sections - 1)
    def _():
        for c in range(chunks):
            for piece in range(SENDS):
                part = h_out.at[pl.ds(c * CHUNK, CHUNK), sends[piece]]
                wait_for(part, h_send_sem.at[c, piece])

    @pl.when(section > 0)
    def _():
        for c in range(chunks):
            for piece in range(SENDS):
                part = g_out.at[pl.ds(c * CHUNK, CHUNK), sends[piece]]
                wait_for(part, g_send_sem.at[c, piece])


def run_chain(tokens, cotangent, gains, w_value, w_out, down, up, criterion, slot_of):
    micro = criterion.shape[0]
    peers = lax.axis_size("dp")
    rows, width = tokens.shape
    value_width = w_out.shape[0]
    chunks = rows // CHUNK
    slots = down.shape[2]
    useful = (down.shape[0] + up.shape[0]) // 2
    packed = (useful + 15) // 16 * 16
    block = rows // micro
    spaces = [pl.BlockSpec(memory_space=pl.ANY)] * 9
    row_buffer = pltpu.VMEM((rows, width), BF16)
    exchange = (micro, peers, packed, LANES)
    return pl.pallas_call(
        chain_kernel,
        out_shape=[
            jax.ShapeDtypeStruct(exchange, BF16),
            jax.ShapeDtypeStruct((micro * criterion.shape[1], slots), F32),
        ],
        in_specs=spaces,
        out_specs=[pl.BlockSpec(memory_space=pl.ANY)] * 2,
        scratch_shapes=[
            pltpu.VMEM(gains.shape, F32),
            pltpu.SMEM(criterion.shape, jnp.int32),
            pltpu.SMEM(slot_of.shape, jnp.int32),
            pltpu.VMEM((micro * criterion.shape[1], slots), F32),
            pltpu.VMEM(w_value.shape, BF16),
            pltpu.VMEM(w_out.shape, BF16),
            pltpu.VMEM(w_out.shape, BF16),
            pltpu.VMEM(w_value.shape, BF16),
            pltpu.VMEM(down.shape, BF16),
            pltpu.VMEM(up.shape, BF16),
            row_buffer,
            row_buffer,
            row_buffer,
            row_buffer,
            row_buffer,
            pltpu.VMEM((rows, LANES), F32),
            pltpu.VMEM((rows, value_width), F32),
            pltpu.VMEM((rows, LANES), F32),
            pltpu.VMEM((rows, value_width), BF16),
            pltpu.VMEM((rows, LANES), BF16),
            pltpu.VMEM((rows, LANES), BF16),
            pltpu.VMEM(exchange, BF16),
            pltpu.VMEM(exchange, BF16),
            pltpu.VMEM((micro, width // 2, LANES), BF16),
            pltpu.VMEM((micro, value_width, LANES), BF16),
            pltpu.VMEM((value_width, LANES), F32),
            pltpu.VMEM(exchange, BF16),
            pltpu.SemaphoreType.DMA((7,)),
            pltpu.SemaphoreType.DMA((2, down.shape[0] // 2 // GROUP)),
            pltpu.SemaphoreType.DMA((chunks, SENDS)),
            pltpu.SemaphoreType.DMA((chunks, SENDS)),
            pltpu.SemaphoreType.DMA((chunks, SENDS)),
            pltpu.SemaphoreType.DMA((chunks, SENDS)),
            pltpu.SemaphoreType.DMA((micro,)),
            pltpu.SemaphoreType.DMA((micro, peers)),
            pltpu.SemaphoreType.DMA((micro,)),
            pltpu.SemaphoreType.DMA((micro,)),
        ],
        compiler_params=pltpu.CompilerParams(
            collective_id=0, has_side_effects=True, vmem_limit_bytes=56 * 1024 * 1024
        ),
        name="chain",
    )(tokens, cotangent, gains, w_value, w_out, down, up, criterion, slot_of)


def place_kernel(picks, parts, down, up, chosen, held, down_out, up_out, pick_sem, load_sem, store_sem):
    pairs = parts.shape[0]
    groups = held.shape[0]
    up_half = up.shape[0] // 2
    half = down.shape[0] // 2
    pick_load = pltpu.make_async_copy(picks, chosen, pick_sem)
    pick_load.start()
    loads = [
        pltpu.make_async_copy(
            parts.at[:, pl.ds(index * GROUP, GROUP)], held.at[index], load_sem.at[index]
        )
        for index in range(groups)
    ]
    for load in loads:
        load.start()
    pick_load.wait()
    one = chosen[...].astype(BF16)
    none = jnp.zeros_like(one)
    pair_of = jnp.concatenate(
        [jnp.concatenate([one, none], axis=1), jnp.concatenate([none, one], axis=1)], axis=0
    )
    slots = chosen.shape[1]
    stores = []
    for index in range(0, groups, 2):
        span = min(2, groups - index)
        for load in loads[index : index + span]:
            load.wait()
        flat = jnp.concatenate([held[index + k] for k in range(span)], axis=0)
        flat = flat.reshape(span * pairs, GROUP * LANES)
        summed = dot_tn(flat, pair_of if span == 2 else one)
        for k in range(span):
            mine = summed[:, k * slots : (k + 1) * slots].reshape(GROUP, 2, LANES // 2, slots)
            for side in range(2):
                if index + k < groups - 1:
                    at = pl.ds(side * half + (index + k) * GROUP, GROUP)
                    source, target = down_out, down
                    down_out[at] = mine[:, side]
                else:
                    at = pl.ds(side * up_half, up_half)
                    source, target = up_out, up
                    up_out[at] = mine[0:up_half, side]
                store = pltpu.make_async_copy(
                    source.at[at], target.at[at], store_sem.at[index + k, side]
                )
                store.start()
                stores.append(store)
    for store in stores:
        store.wait()


def place(picks, parts, feature_rows, value_rows, rank):
    pairs, packed = parts.shape[0:2]
    slots = picks.shape[1]
    groups = packed // GROUP
    down_shape = (feature_rows, rank, slots)
    up_shape = (value_rows, rank, slots)
    return pl.pallas_call(
        place_kernel,
        in_specs=[pl.BlockSpec(memory_space=pltpu.HBM)] * 2,
        out_specs=[pl.BlockSpec(memory_space=pl.ANY)] * 2,
        out_shape=[
            jax.ShapeDtypeStruct(down_shape, F32),
            jax.ShapeDtypeStruct(up_shape, F32),
        ],
        scratch_shapes=[
            pltpu.VMEM((pairs, slots), F32),
            pltpu.VMEM((groups, pairs, GROUP, LANES), BF16),
            pltpu.VMEM(down_shape, F32),
            pltpu.VMEM(up_shape, F32),
            pltpu.SemaphoreType.DMA,
            pltpu.SemaphoreType.DMA((groups,)),
            pltpu.SemaphoreType.DMA((groups, 2)),
        ],
        compiler_params=pltpu.CompilerParams(vmem_limit_bytes=60 * 1024 * 1024),
        name="place",
    )(picks, parts)


def on_device(
    tokens,
    cotangent,
    norm_gain,
    value_weight,
    out_weight,
    adapter_down,
    adapter_up,
    criterion,
    slot_of,
):
    micro, block, width = tokens.shape
    down = jnp.transpose(adapter_down[0], (1, 2, 0))
    up = jnp.transpose(adapter_up[0], (1, 2, 0))
    parts, picks = run_chain(
        tokens.reshape(micro * block, width),
        cotangent.reshape(micro * block, width),
        norm_gain,
        value_weight[0],
        out_weight[0],
        down,
        up,
        criterion,
        slot_of,
    )
    parts = parts.reshape((parts.shape[0] * parts.shape[1],) + parts.shape[2:])
    grad_down, grad_up = place(picks, parts, down.shape[0], up.shape[0], down.shape[1])
    return (jnp.transpose(grad_down, (2, 0, 1))[None], jnp.transpose(grad_up, (2, 0, 1))[None])


def solution(mesh):
    return jax.shard_map(
        on_device,
        mesh=mesh,
        in_specs=(
            P(None, "dp", None),
            P(None, "dp", None),
            P("section", None),
            P("section", None, None),
            P("section", None, None),
            P("section", None, "dp", None),
            P("section", None, "dp", None),
            P(),
            P(),
        ),
        out_specs=(P("section", None, "dp", None), P("section", None, "dp", None)),
        check_vma=False,
    )
```
